512 devices in a mesh: patch: 64 (over y, z), hist: 8 (over x, core).
Axes of the slice: x: 4, y: 8, z: 8, core: 2. Of those that a mesh axis runs over, the one named last changes fastest.
Arguments:
- zblocks: bfloat16 [8, 3072, 128, 128], P('hist', 'patch'), may hold values from -0.078125 to 0.078125
- slot_row: int32 [8, 3072], P('hist', 'patch'), may hold values from 0 to 7
- slot_offset: int32 [8, 3072], P('hist', 'patch'), may hold values from 0 to 8
- slot_delay: int32 [8, 3072], P('hist', 'patch'), may hold values from 0 to 1
- history: bfloat16 [16, 65536, 128], P('hist', 'patch'), may hold values from -6 to 6
- inverse: bfloat16 [65536, 128], P('patch'), may hold values from -0.5 to 0.5
- excite: bfloat16 [4, 65536, 128], P(None, 'patch'), may hold values from -6 to 6
Outputs:
- currents: bfloat16 [4, 65536, 128], P(None, ('patch', 'hist'))
The draws below stay inside these ranges and needn't reach their ends.
All inputs are finite; a program needn't handle non-finite values.
Results may differ from the reference program's by a relative error of at most 0.0035.
Values may be sent and summed in bfloat16 or wider, within the bound.
A program may use at most 64 MiB of HBM per device.

```python
import jax
import jax.numpy as jnp
from jax import lax

BS = 128
NRHS = 128
U = 1024
CAP = 48
KB = 2
R = 4
STEPS = 4
N = 65536
K = 16
SLOTS = 3072
N_HIST = 8


def touch_ends(array, own_key, low, top_value):
    longest = array.shape.index(max(array.shape))
    spots = []
    for shift in (0, 1):
        where = [jax.random.randint(jax.random.fold_in(own_key, axis), (), 0, length) for axis, length in enumerate(array.shape)]
        where[longest] = (where[longest] + shift) % array.shape[longest]
        spots.append(tuple(where))
    return array.at[spots[0]].set(low).at[spots[1]].set(top_value)


def levels(stream_key, shape, cuts, low, high):
    gain = 1.0
    for dim, parts in cuts:
        heights = jax.random.uniform(jax.random.fold_in(jax.random.fold_in(stream_key, 6), dim), (parts,), jnp.float32, low / len(cuts), high / len(cuts))
        gain = gain * jnp.repeat(jnp.exp(heights), shape[dim] // parts).reshape((-1,) + (1,) * (len(shape) - 1 - dim))
    return gain


def normal_values(stream_key, extent, width, reach, pieces=(), held_as=jnp.bfloat16):
    gain = levels(stream_key, extent, pieces, -0.22, 0.18) if pieces else 1.0
    result = jax.random.normal(stream_key, extent, jnp.float32) * width * gain
    return jnp.minimum(jnp.maximum(result, -reach), reach).astype(held_as)


def setup_inputs(seed: int = 0) -> dict:
    streams_of = jax.random.split(jax.random.key(seed), 8)
    return {
        "zblocks": normal_values(streams_of[0], (N_HIST, SLOTS, BS, BS), (BS * CAP * N_HIST * BS // U) ** -0.5, 0.078125, ((0, 8), (1, 64))),
        "slot_row": touch_ends(jax.random.randint(streams_of[1], (N_HIST, SLOTS), 0, U // BS), jax.random.fold_in(streams_of[1], 1), 0, (U // BS) - 1).astype(jnp.int32),
        "slot_offset": touch_ends(jax.random.randint(streams_of[2], (N_HIST, SLOTS), 0, 2 * R + 1), jax.random.fold_in(streams_of[2], 1), 0, 2 * R).astype(jnp.int32),
        "slot_delay": touch_ends(jax.random.randint(streams_of[3], (N_HIST, SLOTS), 0, KB), jax.random.fold_in(streams_of[3], 1), 0, KB - 1).astype(jnp.int32),
        "history": normal_values(streams_of[4], (K, N, NRHS), 1.0, 6.0, ((0, 8), (1, 64))),
        "inverse": normal_values(streams_of[5], (N, BS), BS ** -0.5, 0.5, ((0, 64),)),
        "excite": normal_values(streams_of[6], (STEPS, N, NRHS), 1.0, 6.0, ((1, 64),)),
    }


def reference(zblocks, slot_row, slot_offset, slot_delay, history, inverse, excite):
    nblocks = U // BS
    total_blocks = N // BS
    slot_group = jnp.arange(SLOTS, dtype=jnp.int32) // CAP
    inv_blocks = inverse.reshape(total_blocks, BS, BS).astype(jnp.float32)
    band_state = history
    results = []
    for moment in range(STEPS):
        padded = jnp.pad(band_state, ((0, 0), (R * BS, R * BS), (0, 0)))
        blocked = padded.reshape(K, total_blocks + 2 * R, BS, NRHS)

        def band_sum(band_id):
            row_block = (slot_group * nblocks + slot_row[band_id]).astype(jnp.int32)
            col_block = (row_block + slot_offset[band_id]).astype(jnp.int32)
            delay_idx = (band_id * KB + slot_delay[band_id]).astype(jnp.int32)
            picked = blocked[delay_idx, col_block]
            products = jnp.einsum('sij,sjc->sic', zblocks[band_id].astype(jnp.float32), picked.astype(jnp.float32))
            return jax.ops.segment_sum(products, row_block, num_segments=total_blocks)

        per_band = lax.map(band_sum, jnp.arange(N_HIST, dtype=jnp.int32))
        summed = jnp.sum(per_band, axis=0)
        residual = excite[moment].astype(jnp.float32).reshape(total_blocks, BS, NRHS) - summed
        current = jnp.einsum('bij,bjc->bic', inv_blocks, residual, precision=lax.Precision.HIGHEST).astype(jnp.bfloat16)
        current = current.reshape(N, NRHS)
        results.append(current)
        band_state = jnp.concatenate([current[None], band_state[:-1]], axis=0)
    return jnp.stack(results)
```

```python
import jax
import jax.numpy as jnp
from jax import lax
from jax.experimental import pallas as pl
from jax.experimental.pallas import tpu as pltpu
from jax.sharding import PartitionSpec as P

R = 4
STEPS = 4
ROWS = 8
HALF = ROWS // 2
GROUP = 8
BF16 = jnp.bfloat16
F32 = jnp.float32


def kernel(
    z_hbm, row_ref, off_ref, dly_ref, hist_hbm, inv_hbm, exc_hbm, out_hbm,
    xb0, xb1, xb2, xb3, xb4, xb5, zbuf, sums, stage, twin, mixed, tree, far, near, excv, invv,
    col_s, prev_s, last_s,
    load_sem, halo_send, halo_recv, shift_send, shift_recv,
    twin_send, twin_recv, red_send, red_recv, tree_recv, out_send, out_recv, near_recv,
):
    xb = (xb0, xb1, xb2, xb3, xb4, xb5)
    cap, bs, _ = z_hbm.shape
    p = lax.axis_index("patch")
    h = lax.axis_index("hist")
    p_last = lax.axis_size("patch") - 1
    h_last = lax.axis_size("hist") - 1
    odd = h % 2
    has_left = p > 0
    has_right = p < p_last

    def patch(q):
        return {"patch": q}

    def band(q):
        return {"hist": q}

    def load(i):
        pairs = (
            (hist_hbm.at[1], xb0.at[pl.ds(R, ROWS)]),
            (hist_hbm.at[0], xb1.at[pl.ds(R, ROWS)]),
            (z_hbm, zbuf),
            (inv_hbm, invv),
            (exc_hbm, excv),
        )
        return pltpu.make_async_copy(pairs[i][0], pairs[i][1], load_sem.at[i])

    for i in range(3):
        load(i).start()

    @pl.when(h == 0)
    def _():
        load(3).start()
        load(4).start()

    barrier = pltpu.get_barrier_semaphore()

    def greet(where):
        pl.semaphore_signal(barrier, inc=1, device_id=where, device_id_type=pl.DeviceIdType.MESH)

    @pl.when(has_left)
    def _():
        greet(patch(p - 1))

    @pl.when(has_right)
    def _():
        greet(patch(p + 1))

    @pl.when(h == 0)
    def _():
        for q in range(1, GROUP):
            greet(band(q))

    @pl.when(h > 0)
    def _():
        greet(band(0))

    @pl.when(h > 1)
    def _():
        greet(band(h - 1))

    @pl.when((h > 0) & (h < h_last))
    def _():
        greet(band(h + 1))

    for a, b in ((2, 4), (4, 2), (5, 7), (7, 5)):
        @pl.when(h == a)
        def _(b=b):
            greet(band(b))

    pairs = jnp.where(h == 0, GROUP - 1, 1)
    pairs = pairs + jnp.where(h > 1, 1, 0) + jnp.where((h > 0) & (h < h_last), 1, 0)
    pairs = pairs + jnp.where((h == 2) | (h == 4) | (h == 5) | (h == 7), 1, 0)
    pairs = pairs + jnp.where(has_left, 1, 0) + jnp.where(has_right, 1, 0)
    pl.semaphore_wait(barrier, pairs)

    def remote(src, dst, ssem, rsem, where):
        return pltpu.make_async_remote_copy(
            src_ref=src, dst_ref=dst, send_sem=ssem, recv_sem=rsem,
            device_id=where, device_id_type=pl.DeviceIdType.MESH,
        )

    def to_left(j):
        src = hist_hbm.at[1 - j, pl.ds(0, R)] if j < 2 else xb[j].at[pl.ds(R, R)]
        return remote(src, xb[j].at[pl.ds(R + ROWS, R)], halo_send.at[j, 0], halo_recv.at[j, 1], patch(p - 1))

    def to_right(j):
        src = hist_hbm.at[1 - j, pl.ds(ROWS - R, R)] if j < 2 else xb[j].at[pl.ds(ROWS, R)]
        return remote(src, xb[j].at[pl.ds(0, R)], halo_send.at[j, 1], halo_recv.at[j, 0], patch(p + 1))

    def halo_start(j):
        @pl.when(has_left)
        def _():
            to_left(j).start()

        @pl.when(has_right)
        def _():
            to_right(j).start()

    def halo_wait(j):
        @pl.when(has_left)
        def _():
            to_right(j).wait_recv()

        @pl.when(has_right)
        def _():
            to_left(j).wait_recv()

    def halo_sent(j):
        @pl.when(has_left)
        def _():
            to_left(j).wait_send()

        @pl.when(has_right)
        def _():
            to_right(j).wait_send()

    def shift(j):
        src = hist_hbm.at[1 - j] if j < 2 else xb[j].at[pl.ds(R, ROWS)]
        return remote(src, xb[j + 2].at[pl.ds(R, ROWS)], shift_send.at[j], shift_recv.at[j], band(h + 1))

    def shift_start(j):
        @pl.when(h < h_last)
        def _():
            shift(j).start()

    halo_start(0)
    halo_start(1)
    shift_start(0)
    shift_start(1)

    @pl.when(p == 0)
    def _():
        for j in range(5):
            xb[j][pl.ds(0, R)] = jnp.zeros((R,) + xb[j].shape[1:], BF16)

    @pl.when(p == p_last)
    def _():
        for j in range(5):
            xb[j][pl.ds(R + ROWS, R)] = jnp.zeros((R,) + xb[j].shape[1:], BF16)

    sums[cap] = jnp.zeros(sums.shape[1:], F32)

    def note(s, last):
        row = row_ref[0, s]
        col_s[s] = row + off_ref[0, s]
        before = jnp.int32(cap)
        for r in range(ROWS):
            before = jnp.where(row == r, last[r], before)
        prev_s[s] = before
        return tuple(jnp.where(row == r, s, last[r]) for r in range(ROWS))

    last = lax.fori_loop(0, cap, note, (jnp.int32(cap),) * ROWS)
    for r in range(ROWS):
        last_s[r] = last[r]

    def products(n):
        width = 8 if cap % 8 == 0 else 1

        def some(t, carry):
            for i in range(width):
                s = t * width + i
                col = col_s[s]
                late = dly_ref[0, s]
                x = jnp.where(late == 1, xb[n][col], xb[n + 1][col])
                sums[s] = sums[prev_s[s]] + jnp.dot(zbuf[s], x, preferred_element_type=F32)
            return carry

        lax.fori_loop(0, cap // width, some, 0)

    def row_sum(r):
        return sums[last_s[r]]

    def twin_copy(n):
        return remote(
            stage.at[n, pl.ds(HALF * (1 - odd), HALF)], twin.at[n], twin_send.at[n], twin_recv.at[n],
            band(h + 1 - 2 * odd),
        )

    def near_copy(n):
        return remote(stage.at[n], near.at[n], twin_send.at[n], near_recv.at[n], band(0))

    def far_copy(n, k):
        return remote(mixed.at[n], far.at[n, k], red_send.at[n], red_recv.at[n, k], band(0))

    def tree_copy(n, q):
        return remote(mixed.at[n], tree.at[n], red_send.at[n], tree_recv.at[n], band(q))

    far_from = ((2, 0), (3, 1), (6, 2), (7, 3))

    def out_copy(n, r):
        return remote(xb[n + 2].at[R + r], out_hbm.at[n], out_send.at[n, r], out_recv.at[n], band(r))

    def own_copy(n):
        return pltpu.make_async_copy(xb[n + 2].at[R], out_hbm.at[n], out_send.at[n, 0])

    def solve(n):
        near_copy(n).wait_recv()
        for k in range(4):
            far_copy(n, k).wait_recv()
        for r in range(ROWS):
            total = row_sum(r) + near[n, r]
            for k in ((0, 2) if r < HALF else (1, 3)):
                total = total + far[n, k, r % HALF].astype(F32)
            residual = excv[n, r].astype(F32) - total
            high = residual.astype(BF16)
            low = (residual - high.astype(F32)).astype(BF16)
            inverse = invv[r]
            current = jnp.dot(inverse, high, preferred_element_type=F32) + jnp.dot(
                inverse, low, preferred_element_type=F32
            )
            xb[n + 2][R + r] = current.astype(BF16)
            if n < 3 and r == HALF - 1:
                @pl.when(has_left)
                def _():
                    to_left(n + 2).start()
            if n < 3 and r == ROWS - 1:
                @pl.when(has_right)
                def _():
                    to_right(n + 2).start()
        if n == 0:
            shift(2).start()
        own_copy(n).start()
        for r in range(1, ROWS):
            out_copy(n, r).start()

    def share(n):
        for r in range(ROWS):
            stage[n, r] = row_sum(r)

        @pl.when(h == 1)
        def _():
            near_copy(n).start()

        @pl.when(h > 1)
        def _():
            twin_copy(n).start()

    def merge(n):
        @pl.when(h > 1)
        def _():
            twin_copy(n).wait_recv()

            @pl.when((h == 2) | (h == 7))
            def _():
                tree_copy(n, 0).wait_recv()
                for i in range(HALF):
                    mixed[n, i] = (stage[n, HALF * odd + i] + twin[n, i] + tree[n, i].astype(F32)).astype(BF16)

            @pl.when((h != 2) & (h != 7))
            def _():
                for i in range(HALF):
                    mixed[n, i] = (stage[n, HALF * odd + i] + twin[n, i]).astype(BF16)

            for a, b in ((4, 2), (5, 7)):
                @pl.when(h == a)
                def _(b=b):
                    tree_copy(n, b).start()

            for a, k in far_from:
                @pl.when(h == a)
                def _(k=k):
                    far_copy(n, k).start()

    for i in range(3):
        load(i).wait()

    @pl.when(h == 0)
    def _():
        load(3).wait()
        load(4).wait()

    halo_wait(0)
    halo_wait(1)

    @pl.when(h > 0)
    def _():
        shift(0).wait_recv()
        halo_start(2)
        shift_start(2)

    for n in range(STEPS):
        if n > 0:
            halo_wait(n + 1)
        products(n)

        @pl.when(h == 0)
        def _(n=n):
            solve(n)

        @pl.when(h > 0)
        def _(n=n):
            share(n)
            if n == 0:
                shift(1).wait_recv()
                halo_start(3)
            merge(n)
            if n == 0:
                @pl.when(h > 1)
                def _():
                    shift(2).wait_recv()
                    halo_start(4)
            if n == 2:
                @pl.when(h == 1)
                def _():
                    shift(2).wait_recv()
                    halo_start(4)

    @pl.when(h == 0)
    def _():
        for n in range(STEPS):
            own_copy(n).wait()
            for r in range(1, ROWS):
                out_copy(n, r).wait_send()

    @pl.when(h == 1)
    def _():
        for n in range(STEPS):
            near_copy(n).wait_send()

    @pl.when(h > 1)
    def _():
        for n in range(STEPS):
            twin_copy(n).wait_send()
            far_copy(n, 0).wait_send()

    for j in range(5):
        halo_sent(j)

    @pl.when(h < h_last)
    def _():
        for j in range(3):
            shift(j).wait_send()

    @pl.when(h > 0)
    def _():
        for n in range(STEPS):
            out_copy(n, 0).wait_recv()


def on_device(zblocks, slot_row, slot_offset, slot_delay, history, inverse, excite):
    _, cap, bs, _ = zblocks.shape
    columns = history.shape[2]
    slots = zblocks[0]
    past = history.reshape(history.shape[0], ROWS, bs, columns)
    inv = inverse.reshape(ROWS, bs, bs)
    exc = excite.reshape(STEPS, ROWS, bs, columns)
    any_spec = pl.BlockSpec(memory_space=pl.ANY)
    smem_spec = pl.BlockSpec(memory_space=pltpu.SMEM)
    block = (bs, columns)
    dma = pltpu.SemaphoreType.DMA
    return pl.pallas_call(
        kernel,
        out_shape=jax.ShapeDtypeStruct((STEPS, bs, columns), BF16),
        in_specs=[any_spec, smem_spec, smem_spec, smem_spec, any_spec, any_spec, any_spec],
        out_specs=any_spec,
        scratch_shapes=[pltpu.VMEM((ROWS + 2 * R,) + block, BF16) for _ in range(6)]
        + [
            pltpu.VMEM((cap, bs, bs), BF16),
            pltpu.VMEM((cap + 1,) + block, F32),
            pltpu.VMEM((STEPS, ROWS) + block, F32),
            pltpu.VMEM((STEPS, HALF) + block, F32),
            pltpu.VMEM((STEPS, HALF) + block, BF16),
            pltpu.VMEM((STEPS, HALF) + block, BF16),
            pltpu.VMEM((STEPS, 4, HALF) + block, BF16),
            pltpu.VMEM((STEPS, ROWS) + block, F32),
            pltpu.VMEM((STEPS, ROWS) + block, BF16),
            pltpu.VMEM((ROWS, bs, bs), BF16),
            pltpu.SMEM((cap,), jnp.int32),
            pltpu.SMEM((cap,), jnp.int32),
            pltpu.SMEM((ROWS,), jnp.int32),
            dma((5,)),
            dma((5, 2)),
            dma((5, 2)),
            dma((3,)),
            dma((3,)),
            dma((STEPS,)),
            dma((STEPS,)),
            dma((STEPS,)),
            dma((STEPS, 4)),
            dma((STEPS,)),
            dma((STEPS, ROWS)),
            dma((STEPS,)),
            dma((STEPS,)),
        ],
        compiler_params=pltpu.CompilerParams(
            collective_id=0, has_side_effects=True, vmem_limit_bytes=40 * 1024 * 1024
        ),
    )(slots, slot_row, slot_offset, slot_delay, past, inv, exc)


def solution(mesh):
    return jax.shard_map(
        on_device,
        mesh=mesh,
        in_specs=(
            P("hist", "patch", None, None),
            P("hist", "patch"),
            P("hist", "patch"),
            P("hist", "patch"),
            P("hist", "patch", None),
            P("patch", None),
            P(None, "patch", None),
        ),
        out_specs=P(None, ("patch", "hist"), None),
        check_vma=False,
    )
```

```python
import jax
import jax.numpy as jnp
from jax import lax
from jax.experimental import pallas as pl
from jax.experimental.pallas import tpu as pltpu
from jax.sharding import PartitionSpec as P

R = 4
STEPS = 4
ROWS = 8
HALF = ROWS // 2
GROUP = 8
MARCH = 1
BF16 = jnp.bfloat16
F32 = jnp.float32
ORDER = (0, 4, 1, 5, 2, 6, 3, 7)


def kernel(
    z_hbm, row_hbm, off_hbm, dly_hbm, hist_hbm, inv_hbm, exc_hbm, out_hbm,
    xb0, xb1, xb2, xb3, xb4, xb5, zbuf, sums, stage, twin, mixed, tree, far, excv, invv,
    row_s, off_s, dly_s, col_s, prev_s, last_s,
    load_sem, swap_send, halo_send, halo_recv, shift_send, shift_recv,
    twin_send, twin_recv, red_send, far_recv, tree_recv, out_send, out_recv,
):
    xb = (xb0, xb1, xb2, xb3, xb4, xb5)
    cap = z_hbm.shape[0]
    p = lax.axis_index("patch")
    h = lax.axis_index("hist")
    p_last = lax.axis_size("patch") - 1
    h_last = lax.axis_size("hist") - 1
    odd = h % 2
    first = h < 2
    has_left = p > 0
    has_right = p < p_last

    def when(condition):
        return pl.when(condition)

    def at(patch=p, hist=h):
        return {"patch": patch, "hist": hist}

    barrier = pltpu.get_barrier_semaphore()

    def greet(where):
        pl.semaphore_signal(barrier, inc=1, device_id=where, device_id_type=pl.DeviceIdType.MESH)

    def when_greet(condition, where):
        @when(condition)
        def _():
            greet(where)

    when_greet(has_left, at(patch=p - 1))
    when_greet(has_right, at(patch=p + 1))
    when_greet(has_left & first, at(patch=p - 1, hist=1 - h))
    when_greet(has_right & first, at(patch=p + 1, hist=1 - h))
    lines = ((1, 2), (0, 2, 3, 4, 5, 6, 7), (0, 1, 3), (1, 2, 4, 5), (1, 3, 5), (1, 3, 4, 6, 7), (1, 5, 7), (1, 5, 6))
    met = jnp.int32(0)
    for a, others in enumerate(lines):
        @when(h == a)
        def _(others=others):
            for b in others:
                greet(at(hist=b))

        met = jnp.where(h == a, len(others), met)
    sides = jnp.where(has_left, 1, 0) + jnp.where(has_right, 1, 0)
    met = met + sides * jnp.where(first, 2, 1)

    def remote(src, dst, ssem, rsem, where):
        return pltpu.make_async_remote_copy(
            src_ref=src, dst_ref=dst, send_sem=ssem, recv_sem=rsem,
            device_id=where, device_id_type=pl.DeviceIdType.MESH,
        )

    tables = ((row_hbm, row_s), (off_hbm, off_s), (dly_hbm, dly_s))
    loads = tables + (
        (hist_hbm.at[1], xb0.at[pl.ds(R, ROWS)]),
        (hist_hbm.at[0], xb1.at[pl.ds(R, ROWS)]),
        (z_hbm, zbuf),
    )
    march_loads = ((inv_hbm, invv), (exc_hbm, excv))

    def load(i):
        return pltpu.make_async_copy(loads[i][0], loads[i][1], load_sem.at[i])

    def swap(i):
        return remote(loads[i][0], loads[i][1], swap_send.at[i], load_sem.at[i], at(hist=1 - h))

    def march_load(i):
        return pltpu.make_async_copy(march_loads[i][0], march_loads[i][1], load_sem.at[len(loads) + i])

    def load_wait(i):
        @when(first)
        def _():
            swap(i).wait_recv()

        @when(jnp.logical_not(first))
        def _():
            load(i).wait()

    low, high = pl.ds(0, R), pl.ds(R + ROWS, R)

    def to_left(j, q=None):
        if j < 2:
            src = hist_hbm.at[1 - j, pl.ds(0, R)]
            hist = jnp.where(first, 1 - h, h)
        else:
            src = xb[j].at[pl.ds(R, R)]
            hist = h
        dst = xb[j].at[high]
        if q is not None:
            src, dst = xb[j].at[R + q], xb[j].at[R + ROWS + q]
        return remote(src, dst, halo_send.at[j, 0], halo_recv.at[j, 1], at(patch=p - 1, hist=hist))

    def to_right(j, q=None):
        if j < 2:
            src = hist_hbm.at[1 - j, pl.ds(ROWS - R, R)]
            hist = jnp.where(first, 1 - h, h)
        else:
            src = xb[j].at[pl.ds(ROWS, R)]
            hist = h
        dst = xb[j].at[low]
        if q is not None:
            src, dst = xb[j].at[ROWS + q], xb[j].at[q]
        return remote(src, dst, halo_send.at[j, 1], halo_recv.at[j, 0], at(patch=p + 1, hist=hist))

    def halo_start(j):
        @when(has_left)
        def _():
            to_left(j).start()

        @when(has_right)
        def _():
            to_right(j).start()

    def halo_wait(j):
        @when(has_left)
        def _():
            to_right(j).wait_recv()

        @when(has_right)
        def _():
            to_left(j).wait_recv()

    def halo_sent(j):
        @when(has_left)
        def _():
            to_left(j).wait_send()

        @when(has_right)
        def _():
            to_right(j).wait_send()

    def shift(j):
        src = hist_hbm.at[1 - j] if j < 2 else xb[2].at[pl.ds(R, ROWS)]
        to = h + 1 if j < 2 else jnp.where(h == 1, 0, jnp.where(h == 0, 2, h + 1))
        return remote(src, xb[j + 2].at[pl.ds(R, ROWS)], shift_send.at[j], shift_recv.at[j], at(hist=to))

    def shift_here(j):
        return pltpu.make_async_copy(hist_hbm.at[1 - j], xb[j + 2].at[pl.ds(R, ROWS)], shift_recv.at[j])

    def shift_start(j):
        @when(h == 0)
        def _():
            shift_here(j).start()

        @when((h > 0) & (h < h_last))
        def _():
            shift(j).start()

    def shift_wait(j):
        @when(h == 0)
        def _():
            shift_here(j).wait()

        @when(h > 1)
        def _():
            shift(j).wait_recv()

    @when(jnp.logical_not(first))
    def _():
        for i in range(len(loads)):
            load(i).start()

    @when(h == MARCH)
    def _():
        for i in range(2):
            march_load(i).start()

    pl.semaphore_wait(barrier, met)
    halo_start(0)
    halo_start(1)

    @when(first)
    def _():
        for i in range(len(loads)):
            swap(i).start()

    shift_start(0)
    shift_start(1)

    @when(p == 0)
    def _():
        for j in range(5):
            xb[j][low] = jnp.zeros((R,) + xb[j].shape[1:], BF16)

    @when(p == p_last)
    def _():
        for j in range(5):
            xb[j][high] = jnp.zeros((R,) + xb[j].shape[1:], BF16)

    sums[cap] = jnp.zeros(sums.shape[1:], F32)
    for i in range(3):
        load_wait(i)

    def note(s, last):
        row = row_s[0, s]
        col_s[s] = row + off_s[0, s]
        before = jnp.int32(cap)
        for r in range(ROWS):
            before = jnp.where(row == r, last[r], before)
        prev_s[s] = before
        return tuple(jnp.where(row == r, s, last[r]) for r in range(ROWS))

    last = lax.fori_loop(0, cap, note, (jnp.int32(cap),) * ROWS)
    for r in range(ROWS):
        last_s[r] = last[r]

    def products(n):
        for s in range(cap):
            col = col_s[s]
            x = jnp.where(dly_s[0, s] == 1, xb[n][col], xb[n + 1][col])
            sums[s] = sums[prev_s[s]] + jnp.dot(zbuf[s], x, preferred_element_type=F32)

    def row_sum(r):
        return sums[last_s[r]]

    def twin_copy(n):
        return remote(stage.at[n], twin.at[n], twin_send.at[n], twin_recv.at[n], at(hist=h + 1))

    def far_copy(n, k, r):
        return remote(mixed.at[n, r], far.at[n, k, r], red_send.at[n, r], far_recv.at[n, k, r], at(hist=MARCH))

    def tree_copy(n, r):
        to = 3 if r < HALF else 7
        return remote(mixed.at[n, r], tree.at[n, r % HALF], red_send.at[n, r], tree_recv.at[n, r % HALF], at(hist=to))

    def out_copy(n, r):
        return remote(xb[n + 2].at[R + r], out_hbm.at[n], out_send.at[n, r], out_recv.at[n], at(hist=r))

    def own_copy(n):
        return pltpu.make_async_copy(xb[n + 2].at[R + MARCH], out_hbm.at[n], out_send.at[n, MARCH])

    def solve(n):
        twin_copy(n).wait_recv()
        for r in ORDER:
            for k in range(2):
                far_copy(n, k, r).wait_recv()
            total = row_sum(r) + twin[n, r].astype(F32) + far[n, 0, r].astype(F32) + far[n, 1, r].astype(F32)
            residual = excv[n, r].astype(F32) - total
            coarse = residual.astype(BF16)
            fine = (residual - coarse.astype(F32)).astype(BF16)
            inverse = invv[r]
            current = jnp.dot(inverse, coarse, preferred_element_type=F32) + jnp.dot(
                inverse, fine, preferred_element_type=F32
            )
            xb[n + 2][R + r] = current.astype(BF16)
            if n < STEPS - 1:
                if r < HALF:
                    @when(has_left)
                    def _(r=r):
                        to_left(n + 2, r).start()
                else:
                    @when(has_right)
                    def _(r=r):
                        to_right(n + 2, r - HALF).start()
            elif r != MARCH:
                out_copy(n, r).start()
            else:
                own_copy(n).start()
        if n < STEPS - 1:
            for r in range(ROWS):
                if r != MARCH:
                    out_copy(n, r).start()
            own_copy(n).start()
        if n == 0:
            shift(2).start()

    def share(n):
        for r in range(ROWS):
            stage[n, r] = row_sum(r).astype(BF16)
        twin_copy(n).start()

    def merged(n, r):
        return row_sum(r) + twin[n, r].astype(F32)

    def merge(n):
        twin_copy(n).wait_recv()

        @when(h == 5)
        def _():
            for r in ORDER:
                mixed[n, r] = merged(n, r).astype(BF16)
                tree_copy(n, r).start()

        for a, k, direct, via in ((3, 0, (4, 5, 6, 7), (0, 1, 2, 3)), (7, 1, (0, 1, 2, 3), (4, 5, 6, 7))):
            @when(h == a)
            def _(k=k, direct=direct, via=via):
                for r in direct:
                    mixed[n, r] = merged(n, r).astype(BF16)
                    far_copy(n, k, r).start()
                for r in via:
                    tree_copy(n, r).wait_recv()
                    mixed[n, r] = (merged(n, r) + tree[n, r % HALF].astype(F32)).astype(BF16)
                    far_copy(n, k, r).start()

    for i in range(3, len(loads)):
        load_wait(i)

    @when(h == MARCH)
    def _():
        for i in range(2):
            march_load(i).wait()

    halo_wait(0)
    halo_wait(1)

    @when(h != MARCH)
    def _():
        shift_wait(0)
        halo_start(2)

        @when(h < h_last)
        def _():
            shift(2).start()

    for n in range(STEPS):
        if n > 0:
            halo_wait(n + 1)
        products(n)

        @when(h == MARCH)
        def _(n=n):
            solve(n)

        @when(odd == 0)
        def _(n=n):
            share(n)

        @when((odd == 1) & (h != MARCH))
        def _(n=n):
            merge(n)

        @when(h != MARCH)
        def _(n=n):
            if n == 0:
                shift_wait(1)
                halo_start(3)
            if n == 1:
                @when(h > 1)
                def _():
                    shift(2).wait_recv()
                    halo_start(4)
            if n == 2:
                @when(h == 0)
                def _():
                    shift(2).wait_recv()
                    halo_start(4)

    @when(first)
    def _():
        for i in range(len(loads)):
            swap(i).wait_send()

    @when(odd == 0)
    def _():
        for n in range(STEPS):
            twin_copy(n).wait_send()

    @when((odd == 1) & (h != MARCH))
    def _():
        for n in range(STEPS):
            for r in range(ROWS):
                far_copy(n, 0, r).wait_send()

    for j in range(5):
        halo_sent(j)

    for j in range(3):
        @when((h < h_last) & ((h > 0) if j < 2 else (h >= 0)))
        def _(j=j):
            shift(j).wait_send()

    @when(h == MARCH)
    def _():
        for n in range(STEPS):
            own_copy(n).wait()
            for r in range(ROWS):
                if r != MARCH:
                    out_copy(n, r).wait_send()

    @when(h != MARCH)
    def _():
        for n in range(STEPS):
            out_copy(n, 0).wait_recv()


def on_device(zblocks, slot_row, slot_offset, slot_delay, history, inverse, excite):
    _, cap, bs, _ = zblocks.shape
    columns = history.shape[2]
    slots = zblocks[0]
    past = history.reshape(history.shape[0], ROWS, bs, columns)
    inv = inverse.reshape(ROWS, bs, bs)
    exc = excite.reshape(STEPS, ROWS, bs, columns)
    any_spec = pl.BlockSpec(memory_space=pl.ANY)
    block = (bs, columns)
    dma = pltpu.SemaphoreType.DMA
    return pl.pallas_call(
        kernel,
        out_shape=jax.ShapeDtypeStruct((STEPS, bs, columns), BF16),
        in_specs=[any_spec] * 7,
        out_specs=any_spec,
        scratch_shapes=[pltpu.VMEM((ROWS + 2 * R,) + block, BF16) for _ in range(6)]
        + [
            pltpu.VMEM((cap, bs, bs), BF16),
            pltpu.VMEM((cap + 1,) + block, F32),
            pltpu.VMEM((STEPS, ROWS) + block, BF16),
            pltpu.VMEM((STEPS, ROWS) + block, BF16),
            pltpu.VMEM((STEPS, ROWS) + block, BF16),
            pltpu.VMEM((STEPS, HALF) + block, BF16),
            pltpu.VMEM((STEPS, 2, ROWS) + block, BF16),
            pltpu.VMEM((STEPS, ROWS) + block, BF16),
            pltpu.VMEM((ROWS, bs, bs), BF16),
            pltpu.SMEM((1, cap), jnp.int32),
            pltpu.SMEM((1, cap), jnp.int32),
            pltpu.SMEM((1, cap), jnp.int32),
            pltpu.SMEM((cap,), jnp.int32),
            pltpu.SMEM((cap,), jnp.int32),
            pltpu.SMEM((ROWS,), jnp.int32),
            dma((8,)),
            dma((6,)),
            dma((5, 2)),
            dma((5, 2)),
            dma((3,)),
            dma((3,)),
            dma((STEPS,)),
            dma((STEPS,)),
            dma((STEPS, ROWS)),
            dma((STEPS, 2, ROWS)),
            dma((STEPS, HALF)),
            dma((STEPS, ROWS)),
            dma((STEPS,)),
        ],
        compiler_params=pltpu.CompilerParams(
            collective_id=0, has_side_effects=True, vmem_limit_bytes=60 * 1024 * 1024
        ),
    )(slots, slot_row, slot_offset, slot_delay, past, inv, exc)


def solution(mesh):
    return jax.shard_map(
        on_device,
        mesh=mesh,
        in_specs=(
            P("hist", "patch", None, None),
            P("hist", "patch"),
            P("hist", "patch"),
            P("hist", "patch"),
            P("hist", "patch", None),
            P("patch", None),
            P(None, "patch", None),
        ),
        out_specs=P(None, ("patch", "hist"), None),
        check_vma=False,
    )
```

```python
import jax
import jax.numpy as jnp
from jax import lax
from jax.experimental import pallas as pl
from jax.experimental.pallas import tpu as pltpu
from jax.sharding import PartitionSpec as P

R = 4
STEPS = 4
ROWS = 8
HALF = ROWS // 2
GROUP = 8
MARCH = 1
BF16 = jnp.bfloat16
F32 = jnp.float32
ORDER = (0, 4, 1, 5, 2, 6, 3, 7)
LAST_ORDER = (4, 5, 6, 7, 2, 3, 0, 1)


def kernel(
    z_hbm, row_hbm, off_hbm, dly_hbm, hist_hbm, inv_hbm, exc_hbm, out_ref,
    xa, xb2, xb3, xb4, cur3, zbuf, sums, stage, twin, mixed, tree, far, excv, invv,
    row_s, off_s, dly_s, col_s, prev_s, last_s,
    go_sem, load_sem, swap_send, halo_send, halo_recv, shift_send, shift_recv,
    twin_send, twin_recv, red_send, far_first, far_recv, tree_first, tree_recv, out_send, own_send, out_recv,
):
    xb = (None, None, xb2, xb3, xb4)
    cap = z_hbm.shape[0]
    p = lax.axis_index("patch")
    h = lax.axis_index("hist")
    p_last = lax.axis_size("patch") - 1
    h_last = lax.axis_size("hist") - 1
    odd = h % 2
    first = h < 2
    later = h > 1
    lower = (h == MARCH) | (later & (odd == 0))
    upper = jnp.logical_not(lower)
    march = h == MARCH
    even = later & (odd == 0)
    gate = later & (odd == 1)
    has_left = p > 0
    has_right = p < p_last
    when = pl.when

    def at(patch=p, hist=h):
        return {"patch": patch, "hist": hist}

    barrier = pltpu.get_barrier_semaphore()

    def greet(where):
        pl.semaphore_signal(barrier, inc=1, device_id=where, device_id_type=pl.DeviceIdType.MESH)

    for side, q in ((has_left, p - 1), (has_right, p + 1)):
        @when(side & (h > 0))
        def _(q=q):
            greet(at(patch=q))

        @when(side & first)
        def _(q=q):
            greet(at(patch=q, hist=1 - h))

    lines = (
        (1, 2), (0, 2, 3, 4, 5, 6, 7), (0, 1, 3, 4), (1, 2, 4, 5),
        (1, 2, 3, 5, 6), (1, 3, 4, 6, 7), (1, 4, 5, 7), (1, 5, 6),
    )
    met = jnp.int32(0)
    for a, others in enumerate(lines):
        @when(h == a)
        def _(others=others):
            for b in others:
                greet(at(hist=b))

        met = jnp.where(h == a, len(others), met)
    sides = jnp.where(has_left, 1, 0) + jnp.where(has_right, 1, 0)
    met = met + sides * jnp.where(march, 2, 1)

    def remote(src, dst, ssem, rsem, where):
        return pltpu.make_async_remote_copy(
            src_ref=src, dst_ref=dst, send_sem=ssem, recv_sem=rsem,
            device_id=where, device_id_type=pl.DeviceIdType.MESH,
        )

    loads = (
        (row_hbm, row_s), (off_hbm, off_s), (dly_hbm, dly_s),
        (hist_hbm, xa.at[:, pl.ds(R, ROWS)]), (z_hbm, zbuf),
    )
    march_loads = ((inv_hbm, invv), (exc_hbm, excv))

    def load(i):
        return pltpu.make_async_copy(loads[i][0], loads[i][1], load_sem.at[i])

    def swap(i):
        return remote(loads[i][0], loads[i][1], swap_send.at[i], load_sem.at[i], at(hist=1 - h))

    def march_load(i):
        return pltpu.make_async_copy(march_loads[i][0], march_loads[i][1], load_sem.at[len(loads) + i])

    def load_wait(i):
        @when(first)
        def _():
            swap(i).wait_recv()

        @when(later)
        def _():
            load(i).wait()

    low, mid, high = pl.ds(0, R), pl.ds(R, ROWS), pl.ds(R + ROWS, R)

    partner = jnp.where(first, 1 - h, h)

    def own_left(i):
        return remote(
            hist_hbm.at[i, pl.ds(0, R)], xa.at[i, high], halo_send.at[0, i], halo_recv.at[0, 1], at(p - 1, partner)
        )

    def own_right(i):
        return remote(
            hist_hbm.at[i, pl.ds(ROWS - R, R)], xa.at[i, low], halo_send.at[1, i], halo_recv.at[0, 0], at(p + 1, partner)
        )

    def own_start():
        for i in (1, 0):
            @when(has_left)
            def _(i=i):
                own_left(i).start()

            @when(has_right)
            def _(i=i):
                own_right(i).start()

    def own_sent(i):
        @when(has_left)
        def _():
            own_left(i).wait_send()

        @when(has_right)
        def _():
            own_right(i).wait_send()

    def own_wait():
        @when(has_left)
        def _():
            remote(hist_hbm.at[:, pl.ds(0, R)], xa.at[:, low], halo_send.at[0, 0], halo_recv.at[0, 0], at(p - 1)).wait_recv()

        @when(has_right)
        def _():
            remote(hist_hbm.at[:, pl.ds(0, R)], xa.at[:, high], halo_send.at[0, 0], halo_recv.at[0, 1], at(p + 1)).wait_recv()

    def to_left(j, q=None):
        src, dst = (xb[j].at[pl.ds(R, R)], xb[j].at[high]) if q is None else (xb[j].at[R + q], xb[j].at[R + ROWS + q])
        return remote(src, dst, halo_send.at[0, j % 2], halo_recv.at[j - 1, 1], at(p - 1))

    def to_right(j, q=None):
        src, dst = (xb[j].at[pl.ds(ROWS, R)], xb[j].at[low]) if q is None else (xb[j].at[ROWS + q], xb[j].at[q])
        return remote(src, dst, halo_send.at[1, j % 2], halo_recv.at[j - 1, 0], at(p + 1))

    def halo_start(j):
        @when(has_left)
        def _():
            to_left(j).start()

        @when(has_right)
        def _():
            to_right(j).start()

    def halo_wait(j):
        @when(has_left)
        def _():
            to_right(j).wait_recv()

        @when(has_right)
        def _():
            to_left(j).wait_recv()

    def halo_sent(j):
        @when(has_left)
        def _():
            to_left(j).wait_send()

        @when(has_right)
        def _():
            to_right(j).wait_send()

    def cross(j):
        src, to = (hist_hbm.at[3 - j], h + 1) if j < 4 else (hist_hbm.at[1], h + 2)
        return remote(src, xb[j].at[mid], shift_send.at[j - 2], shift_recv.at[j - 2], at(hist=to))

    def inside(j):
        src = xa.at[3 - j] if j < 4 else xb2
        return remote(src, xb[j], shift_send.at[j - 2], shift_recv.at[j - 2], at(hist=h + 1 - 2 * odd))

    @when(later)
    def _():
        for i in range(len(loads)):
            load(i).start()

    @when(march)
    def _():
        for i in range(2):
            march_load(i).start()

    pl.semaphore_wait(barrier, met)

    @when(first | even)
    def _():
        own_start()

    @when((odd == 1) & (h < h_last))
    def _():
        cross(2).start()
        cross(3).start()

    @when(first)
    def _():
        for i in range(len(loads)):
            swap(i).start()

    @when(even)
    def _():
        own_sent(1)
        pl.semaphore_signal(go_sem, inc=1, device_id=at(hist=h + 1), device_id_type=pl.DeviceIdType.MESH)

    @when(gate)
    def _():
        pl.semaphore_wait(go_sem, 1)
        own_start()

    for edge, where in ((p == 0, low), (p == p_last, high)):
        @when(edge)
        def _(where=where):
            for i in range(2):
                xa[i, where] = jnp.zeros((R,) + xb2.shape[1:], BF16)

        @when(edge & lower)
        def _(where=where):
            for j in (2, 3, 4):
                xb[j][where] = jnp.zeros((R,) + xb2.shape[1:], BF16)

    sums[cap] = jnp.zeros(sums.shape[1:], F32)
    for i in range(3):
        load_wait(i)

    def note(s, last):
        row = row_s[0, s]
        col_s[s] = row + off_s[0, s]
        before = jnp.int32(cap)
        for r in range(ROWS):
            before = jnp.where(row == r, last[r], before)
        prev_s[s] = before
        return tuple(jnp.where(row == r, s, last[r]) for r in range(ROWS))

    last = lax.fori_loop(0, cap, note, (jnp.int32(cap),) * ROWS)
    for r in range(ROWS):
        last_s[r] = last[r]

    def products(n):
        for s in range(cap):
            col = col_s[s]
            delay = dly_s[0, s]
            if n == 0:
                x = xa[delay, col]
            else:
                x = jnp.where(delay == 1, xa[0, col] if n == 1 else xb[n][col], xb[n + 1][col])
            sums[s] = sums[prev_s[s]] + jnp.dot(zbuf[s], x, preferred_element_type=F32)

    def row_sum(r):
        return sums[last_s[r]]

    def twin_copy(n):
        return remote(stage.at[n], twin.at[n], twin_send, twin_recv.at[n], at(hist=h + 1))

    def far_copy(n, k, r):
        rsem = far_first.at[k, r % HALF] if n == 0 else far_recv.at[n - 1, k]
        return remote(mixed.at[n, r], far.at[n, k, r], red_send, rsem, at(hist=MARCH))

    def tree_copy(n, r):
        rsem = tree_first.at[r % HALF] if n == 0 else tree_recv.at[n - 1]
        return remote(mixed.at[n, r], tree.at[n, r % HALF], red_send, rsem, at(hist=3 if r < HALF else 7))

    def mixed_sent(n):
        remote(mixed.at[n], mixed.at[n], red_send, red_send, at(hist=MARCH)).wait_send()

    def far_wait(n, r):
        for k in range(2):
            if n == 0 and r < HALF:
                remote(mixed.at[0, pl.ds(0, 2)], far.at[0, k, pl.ds(0, 2)], red_send, far_first.at[k, r], at()).wait_recv()
            if n > 0 and r == 0:
                remote(mixed.at[n], far.at[n, k], red_send, far_recv.at[n - 1, k], at()).wait_recv()

    def tree_wait(n, r):
        if n == 0:
            tree_copy(n, r).wait_recv()
        elif r % HALF == 0:
            remote(mixed.at[n, pl.ds(0, HALF)], tree.at[n], red_send, tree_recv.at[n - 1], at()).wait_recv()

    def current_ref(n, r):
        return cur3.at[r] if n == STEPS - 1 else xb[n + 2].at[R + r]

    def out_copy(n, r):
        return remote(current_ref(n, r), out_ref.at[n], out_send, out_recv, at(hist=r))

    def own_copy(n):
        return pltpu.make_async_copy(current_ref(n, MARCH), out_ref.at[n], own_send)

    def out_start(n, r):
        if r == MARCH:
            own_copy(n).start()
        else:
            out_copy(n, r).start()

    def solve(n):
        twin_copy(n).wait_recv()
        if n == 0:
            own_sent(0)
            own_sent(1)
        if n == 2:
            halo_sent(2)
        if n > 0:
            far_wait(n, 0)
        for r in ORDER if n < STEPS - 1 else LAST_ORDER:
            if n == 0:
                far_wait(0, r)
            total = row_sum(r) + twin[n, r].astype(F32) + far[n, 0, r].astype(F32) + far[n, 1, r].astype(F32)
            residual = excv[n, r].astype(F32) - total
            coarse = residual.astype(BF16)
            fine = (residual - coarse.astype(F32)).astype(BF16)
            inverse = invv[r]
            current = jnp.dot(inverse, coarse, preferred_element_type=F32) + jnp.dot(
                inverse, fine, preferred_element_type=F32
            )
            current_ref(n, r)[...] = current.astype(BF16)
            if n == STEPS - 1:
                out_start(n, r)
            elif r < HALF:
                @when(has_left)
                def _(r=r):
                    to_left(n + 2, r).start()
            else:
                @when(has_right)
                def _(r=r):
                    to_right(n + 2, r - HALF).start()
        if n < STEPS - 1:
            for r in range(ROWS):
                out_start(n, r)

    def share(n):
        if n > 0:
            twin_copy(n - 1).wait_send()
        for r in range(ROWS):
            stage[n, r] = row_sum(r).astype(BF16)
        twin_copy(n).start()

    def merged(n, r):
        return row_sum(r) + twin[n, r].astype(F32)

    def merge(n):
        twin_copy(n).wait_recv()
        if n > 0:
            mixed_sent(n - 1)

        @when(h == 5)
        def _():
            for r in ORDER:
                mixed[n, r] = merged(n, r).astype(BF16)
                tree_copy(n, r).start()

        for a, k, direct, via in ((3, 0, (4, 5, 6, 7), (0, 1, 2, 3)), (7, 1, (0, 1, 2, 3), (4, 5, 6, 7))):
            @when(h == a)
            def _(k=k, direct=direct, via=via):
                for r in direct:
                    mixed[n, r] = merged(n, r).astype(BF16)
                    far_copy(n, k, r).start()
                for r in via:
                    tree_wait(n, r)
                    mixed[n, r] = (merged(n, r) + tree[n, r % HALF].astype(F32)).astype(BF16)
                    far_copy(n, k, r).start()

    for i in range(3, len(loads)):
        load_wait(i)

    @when(march)
    def _():
        for i in range(2):
            march_load(i).wait()

    own_wait()

    @when(march)
    def _():
        inside(2).start()
        inside(3).start()

    for n in range(STEPS):
        if n > 0:
            @when(lower)
            def _(n=n):
                halo_wait(n + 1)

            @when(upper)
            def _(n=n):
                inside(n + 1).wait_recv()

        products(n)

        @when(march)
        def _(n=n):
            solve(n)
            if n == 1:
                inside(4).start()

        @when(odd == 0)
        def _(n=n):
            share(n)

        @when(gate)
        def _(n=n):
            merge(n)

        if n == 0:
            @when(even)
            def _():
                inside(2).start()
                inside(3).start()
                cross(2).wait_recv()
                own_sent(0)
                halo_start(2)

            @when((odd == 0) & (h + 2 <= h_last))
            def _():
                cross(4).start()

            @when(even)
            def _():
                cross(3).wait_recv()
                halo_start(3)

        if n == 1:
            @when(even)
            def _():
                inside(4).start()
                cross(4).wait_recv()
                halo_sent(2)
                halo_start(4)

    @when(first)
    def _():
        for i in range(len(loads)):
            swap(i).wait_send()

    @when((h == 0) | gate)
    def _():
        own_sent(0)
        own_sent(1)

    @when(lower)
    def _():
        halo_sent(3)
        halo_sent(4)
        for j in (2, 3, 4):
            inside(j).wait_send()

    @when((odd == 1) & (h < h_last))
    def _():
        cross(2).wait_send()
        cross(3).wait_send()

    @when((odd == 0) & (h + 2 <= h_last))
    def _():
        cross(4).wait_send()

    @when(odd == 0)
    def _():
        twin_copy(STEPS - 1).wait_send()

    @when(gate)
    def _():
        mixed_sent(STEPS - 1)

    @when(march)
    def _():
        pltpu.make_async_copy(stage.at[0, pl.ds(0, STEPS)], out_ref, own_send).wait()
        remote(mixed.at[:, pl.ds(0, ROWS - 1)], mixed.at[:, pl.ds(0, ROWS - 1)], out_send, out_recv, at(hist=0)).wait_send()

    @when(jnp.logical_not(march))
    def _():
        remote(stage.at[0, pl.ds(0, STEPS)], out_ref, out_send, out_recv, at(hist=MARCH)).wait_recv()


def on_device(zblocks, slot_row, slot_offset, slot_delay, history, inverse, excite):
    _, cap, bs, _ = zblocks.shape
    columns = history.shape[2]
    slots = zblocks[0]
    past = history.reshape(history.shape[0], ROWS, bs, columns)
    inv = inverse.reshape(ROWS, bs, bs)
    exc = excite.reshape(STEPS, ROWS, bs, columns)
    operands = (slots, slot_row, slot_offset, slot_delay, past, inv, exc)
    any_spec = pl.BlockSpec(memory_space=pl.ANY)
    block = (bs, columns)
    dma = pltpu.SemaphoreType.DMA
    return pl.pallas_call(
        kernel,
        out_shape=pltpu.VMEM((STEPS, bs, columns), BF16),
        in_specs=[any_spec] * 7,
        out_specs=any_spec,
        scratch_shapes=[pltpu.VMEM((2, ROWS + 2 * R) + block, BF16)]
        + [pltpu.VMEM((ROWS + 2 * R,) + block, BF16) for _ in range(3)]
        + [
            pltpu.VMEM((ROWS,) + block, BF16),
            pltpu.VMEM((cap, bs, bs), BF16),
            pltpu.VMEM((cap + 1,) + block, F32),
            pltpu.VMEM((STEPS, ROWS) + block, BF16),
            pltpu.VMEM((STEPS, ROWS) + block, BF16),
            pltpu.VMEM((STEPS, ROWS) + block, BF16),
            pltpu.VMEM((STEPS, HALF) + block, BF16),
            pltpu.VMEM((STEPS, 2, ROWS) + block, BF16),
            pltpu.VMEM((STEPS, ROWS) + block, BF16),
            pltpu.VMEM((ROWS, bs, bs), BF16),
            pltpu.SMEM((1, cap), jnp.int32),
            pltpu.SMEM((1, cap), jnp.int32),
            pltpu.SMEM((1, cap), jnp.int32),
            pltpu.SMEM((cap,), jnp.int32),
            pltpu.SMEM((cap,), jnp.int32),
            pltpu.SMEM((ROWS,), jnp.int32),
            pltpu.SemaphoreType.REGULAR,
            dma((7,)),
            dma((5,)),
            dma((2, 2)),
            dma((4, 2)),
            dma((3,)),
            dma((3,)),
            dma,
            dma((STEPS,)),
            dma,
            dma((2, HALF)),
            dma((STEPS - 1, 2)),
            dma((HALF,)),
            dma((STEPS - 1,)),
            dma,
            dma,
            dma,
        ],
        compiler_params=pltpu.CompilerParams(
            collective_id=0, has_side_effects=True, vmem_limit_bytes=60 * 1024 * 1024
        ),
    )(*[pltpu.with_memory_space_constraint(v, pltpu.HBM) for v in operands])


def solution(mesh):
    return jax.shard_map(
        on_device,
        mesh=mesh,
        in_specs=(
            P("hist", "patch", None, None),
            P("hist", "patch"),
            P("hist", "patch"),
            P("hist", "patch"),
            P("hist", "patch", None),
            P("patch", None),
            P(None, "patch", None),
        ),
        out_specs=P(None, ("patch", "hist"), None),
        check_vma=False,
    )
```

```python
import jax
import jax.numpy as jnp
from jax import lax
from jax.experimental import pallas as pl
from jax.experimental.pallas import tpu as pltpu
from jax.sharding import PartitionSpec as P

R = 4
STEPS = 4
ROWS = 8
HALF = ROWS // 2
GROUP = 8
MARCH = 1
FINE = 2
BF16 = jnp.bfloat16
F32 = jnp.float32
PARTS = ((0, 5), (1, 6), (2, 7), (3, 4))
ORDER = tuple(r for part in PARTS for r in part)
LAST_ORDER = (4, 5, 6, 7, 2, 3, 0, 1)
LEFT = tuple((r, c) for r in range(HALF) for c in range(r, R))
RIGHT = tuple((r, c) for r in range(HALF, ROWS) for c in range(R + ROWS, r + 2 * R + 1))
PLACES = LEFT + RIGHT
WIDTH = ROWS + 2 * R
BY_ONE = (0, 1, 2, 3, 4)
BY_THREE = (5, 6, 7)


def kernel(
    z_hbm, row_hbm, off_hbm, dly_hbm, hist_hbm, inv_hbm, exc_hbm, out_ref,
    xa, xb2, xb3, xb4, mid_only, cur3, dense, zbuf, sums, stage, twin, mixed, tree, far, base, excv, invv,
    row_s, off_s, dly_s, col_s, prev_s, last_s, same_s, place_s,
    go_sem, load_sem, swap_send, halo_send, halo_recv, shift_send, shift_recv,
    twin_send, twin_recv, red_send, far_first, far_recv, tree_first, tree_recv, out_send, own_send, out_recv,
):
    xb = (None, None, xb2, xb3, xb4)
    cap = z_hbm.shape[0]
    p = lax.axis_index("patch")
    h = lax.axis_index("hist")
    p_last = lax.axis_size("patch") - 1
    h_last = lax.axis_size("hist") - 1
    odd = h % 2
    first = h < 2
    later = h > 1
    lower = (h == MARCH) | (later & (odd == 0))
    upper = jnp.logical_not(lower)
    march = h == MARCH
    even = later & (odd == 0)
    gate = later & (odd == 1)
    has_left = p > 0
    has_right = p < p_last
    far_right = p % 8 == 7
    when = pl.when

    def at(patch=p, hist=h):
        return {"patch": patch, "hist": hist}

    barrier = pltpu.get_barrier_semaphore()

    def greet(where):
        pl.semaphore_signal(barrier, inc=1, device_id=where, device_id_type=pl.DeviceIdType.MESH)

    for side, q in ((has_left, p - 1), (has_right, p + 1)):
        @when(side & (h > 0))
        def _(q=q):
            greet(at(patch=q))

        @when(side & first)
        def _(q=q):
            greet(at(patch=q, hist=1 - h))

    lines = (
        (1, 2), (0, 2, 3, 4, 5, 6, 7), (0, 1, 3, 4), (1, 2, 4, 5),
        (1, 2, 3, 5, 6), (1, 3, 4, 6, 7), (1, 4, 5, 7), (1, 5, 6),
    )
    met = jnp.int32(0)
    for a, others in enumerate(lines):
        @when(h == a)
        def _(others=others):
            for b in others:
                greet(at(hist=b))

        met = jnp.where(h == a, len(others), met)
    sides = jnp.where(has_left, 1, 0) + jnp.where(has_right, 1, 0)
    met = met + sides * jnp.where(march, 2, 1)

    def remote(src, dst, ssem, rsem, where):
        return pltpu.make_async_remote_copy(
            src_ref=src, dst_ref=dst, send_sem=ssem, recv_sem=rsem,
            device_id=where, device_id_type=pl.DeviceIdType.MESH,
        )

    loads = (
        (row_hbm, row_s), (off_hbm, off_s), (dly_hbm, dly_s),
        (hist_hbm, xa.at[:, pl.ds(R, ROWS)]), (z_hbm, zbuf),
    )
    march_loads = ((inv_hbm, invv), (exc_hbm, excv))

    def load(i):
        return pltpu.make_async_copy(loads[i][0], loads[i][1], load_sem.at[i])

    def swap(i):
        return remote(loads[i][0], loads[i][1], swap_send.at[i], load_sem.at[i], at(hist=1 - h))

    def march_load(i):
        return pltpu.make_async_copy(march_loads[i][0], march_loads[i][1], load_sem.at[len(loads) + i])

    def load_wait(i):
        @when(first)
        def _():
            swap(i).wait_recv()

        @when(later)
        def _():
            load(i).wait()

    low, mid, high = pl.ds(0, R), pl.ds(R, ROWS), pl.ds(R + ROWS, R)

    partner = jnp.where(first, 1 - h, h)

    pieces = ((1, R // 2, R // 2), (0, 0, R), (1, 0, R // 2))

    def own_left(t):
        i, first_block, blocks = pieces[t]
        src = hist_hbm.at[i, pl.ds(first_block, blocks)]
        dst = xa.at[i, pl.ds(R + ROWS + first_block, blocks)]
        return remote(src, dst, halo_send.at[0, t // 2], halo_recv.at[0, 1], at(p - 1, partner))

    def own_right(t):
        i, first_block, blocks = pieces[t]
        src = hist_hbm.at[i, pl.ds(ROWS - R + first_block, blocks)]
        dst = xa.at[i, pl.ds(first_block, blocks)]
        return remote(src, dst, halo_send.at[1, t // 2], halo_recv.at[0, 0], at(p + 1, partner))

    def own_start():
        for t in (2, 0, 1):
            @when(has_left)
            def _(t=t):
                own_left(t).start()

            @when(has_right)
            def _(t=t):
                own_right(t).start()

    def own_sent(t):
        some = xb2.at[pl.ds(0, R // 2 if t == 1 else R + R // 2)]
        for side, present in enumerate((has_left, has_right)):
            @when(present)
            def _(side=side):
                remote(some, some, halo_send.at[side, t], halo_recv.at[0, 0], at()).wait_send()

    def own_wait():
        @when(has_left)
        def _():
            remote(hist_hbm.at[:, pl.ds(0, R)], xa.at[:, low], halo_send.at[0, 0], halo_recv.at[0, 0], at(p - 1)).wait_recv()

        @when(has_right)
        def _():
            remote(hist_hbm.at[:, pl.ds(0, R)], xa.at[:, high], halo_send.at[0, 0], halo_recv.at[0, 1], at(p + 1)).wait_recv()

    def to_left(j, q=None):
        src, dst = (xb[j].at[pl.ds(R, R)], xb[j].at[high]) if q is None else (xb[j].at[R + q], xb[j].at[R + ROWS + q])
        return remote(src, dst, halo_send.at[0, j % 2], halo_recv.at[j - 1, 1], at(p - 1))

    def to_right(j, q=None):
        src, dst = (xb[j].at[pl.ds(ROWS, R)], xb[j].at[low]) if q is None else (xb[j].at[ROWS + q], xb[j].at[q])
        return remote(src, dst, halo_send.at[1, j % 2], halo_recv.at[j - 1, 0], at(p + 1))

    def halo_start(j):
        @when(has_left)
        def _():
            to_left(j).start()

        @when(has_right)
        def _():
            to_right(j).start()

    def halo_wait(j):
        @when(has_left)
        def _():
            to_right(j).wait_recv()

        @when(has_right)
        def _():
            to_left(j).wait_recv()

    def halo_sent(j):
        @when(has_left)
        def _():
            to_left(j).wait_send()

        @when(has_right)
        def _():
            to_right(j).wait_send()

    def cross(j):
        src, to = (hist_hbm.at[3 - j], h + 1) if j < 4 else (hist_hbm.at[1], h + 2)
        return remote(src, xb[j].at[mid], shift_send.at[j - 2], shift_recv.at[j - 2], at(hist=to))

    def inside(j):
        src = xa.at[3 - j] if j < 4 else xb2
        return remote(src, xb[j], shift_send.at[j - 2], shift_recv.at[j - 2], at(hist=h + 1 - 2 * odd))

    @when(later)
    def _():
        for i in range(len(loads)):
            load(i).start()

    @when(march)
    def _():
        for i in range(2):
            march_load(i).start()

    pl.semaphore_wait(barrier, met)

    @when(first | even)
    def _():
        own_start()

    @when((odd == 1) & (h < h_last))
    def _():
        cross(2).start()
        cross(3).start()

    @when(first)
    def _():
        for i in range(len(loads)):
            swap(i).start()

    @when(even)
    def _():
        own_sent(1)
        pl.semaphore_signal(go_sem, inc=1, device_id=at(hist=h + 1), device_id_type=pl.DeviceIdType.MESH)

    @when(gate)
    def _():
        pl.semaphore_wait(go_sem, 1)
        own_start()

    for edge, where in ((p == 0, low), (p == p_last, high)):
        @when(edge)
        def _(where=where):
            for i in range(2):
                xa[i, where] = jnp.zeros((R,) + xb2.shape[1:], BF16)

        @when(edge & lower)
        def _(where=where):
            for j in (2, 3, 4):
                xb[j][where] = jnp.zeros((R,) + xb2.shape[1:], BF16)

    sums[cap] = jnp.zeros(sums.shape[1:], F32)
    for i in range(3):
        load_wait(i)

    def note(s, last):
        row = row_s[0, s]
        col_s[s] = row + off_s[0, s]
        before = jnp.int32(cap)
        for r in range(ROWS):
            before = jnp.where(row == r, last[r], before)
        prev_s[s] = before
        return tuple(jnp.where(row == r, s, last[r]) for r in range(ROWS))

    last = lax.fori_loop(0, cap, note, (jnp.int32(cap),) * ROWS)
    for r in range(ROWS):
        last_s[r] = last[r]

    @when(march)
    def _():
        def note_place(s, seen):
            place = jnp.where(dly_s[0, s] == 0, row_s[0, s] * WIDTH + col_s[s], -1)
            before = jnp.int32(cap)
            for k, (r, c) in enumerate(PLACES):
                before = jnp.where(place == r * WIDTH + c, seen[k], before)
            same_s[s] = before
            return tuple(jnp.where(place == r * WIDTH + c, s, seen[k]) for k, (r, c) in enumerate(PLACES))

        seen = lax.fori_loop(0, cap, note_place, (jnp.int32(cap),) * len(PLACES))
        for k in range(len(PLACES)):
            place_s[k] = seen[k]
        mid_only[low] = jnp.zeros((R,) + xb2.shape[1:], BF16)
        mid_only[high] = jnp.zeros((R,) + xb2.shape[1:], BF16)

    def products(n, newest=None):
        for s in range(cap):
            col = col_s[s]
            delay = dly_s[0, s]
            if n == 0:
                x = xa[delay, col]
            else:
                new = xb[n + 1][col] if newest is None else newest[col]
                x = jnp.where(delay == 1, xa[0, col] if n == 1 else xb[n][col], new)
            sums[s] = sums[prev_s[s]] + jnp.dot(zbuf[s], x, preferred_element_type=F32)

    def row_sum(r):
        return sums[last_s[r]]

    def twin_copy(n):
        return remote(stage.at[n], twin.at[n], twin_send, twin_recv.at[n], at(hist=h + 1))

    def part_of(r):
        return [r in part for part in PARTS].index(True)

    def far_copy(n, k, r):
        rsem = far_first.at[n, k, part_of(r)] if n < FINE else far_recv.at[n - FINE, k]
        return remote(mixed.at[n, r], far.at[n, k, r], red_send, rsem, at(hist=MARCH))

    def tree_copy(n, r):
        to, i = (3, r) if r in BY_ONE else (7, r - BY_THREE[0])
        rsem = tree_first.at[n, i] if n < FINE else tree_recv.at[n - FINE]
        return remote(mixed.at[n, r], tree.at[n, i], red_send, rsem, at(hist=to))

    def mixed_sent(n):
        remote(mixed.at[n], mixed.at[n], red_send, red_send, at(hist=MARCH)).wait_send()

    def far_wait(n, part):
        for k in range(2):
            if n < FINE:
                src, dst, rsem = mixed.at[n, pl.ds(0, 2)], far.at[n, k, pl.ds(0, 2)], far_first.at[n, k, part]
            else:
                src, dst, rsem = mixed.at[n], far.at[n, k], far_recv.at[n - FINE, k]
            remote(src, dst, red_send, rsem, at()).wait_recv()

    def tree_wait(n, rows, r):
        if n < FINE:
            tree_copy(n, r).wait_recv()
        elif r == rows[0]:
            some = pl.ds(0, len(rows))
            remote(mixed.at[n, some], tree.at[n, some], red_send, tree_recv.at[n - FINE], at()).wait_recv()

    def current_ref(n, r):
        return cur3.at[r] if n == STEPS - 1 else xb[n + 2].at[R + r]

    def out_copy(n, r):
        return remote(current_ref(n, r), out_ref.at[n], out_send, out_recv, at(hist=r))

    def own_copy(n):
        return pltpu.make_async_copy(current_ref(n, MARCH), out_ref.at[n], own_send)

    def out_start(n, r):
        if r == MARCH:
            own_copy(n).start()
        else:
            out_copy(n, r).start()

    def fold():
        for slot in range(cap):
            folded = jnp.dot(invv[row_s[0, slot]], zbuf[slot], preferred_element_type=F32)
            zbuf[slot] = folded.astype(BF16)
            sums[slot] = sums[same_s[slot]] + folded
        for k in range(len(PLACES)):
            dense[k] = sums[place_s[k]].astype(BF16)

    def solved(n, r):
        total = twin[n, r].astype(F32) + far[n, 0, r].astype(F32) + far[n, 1, r].astype(F32)
        residual = excv[n, r].astype(F32) - total
        coarse = residual.astype(BF16)
        fine = (residual - coarse.astype(F32)).astype(BF16)
        return jnp.dot(invv[r], coarse, preferred_element_type=F32) + jnp.dot(
            invv[r], fine, preferred_element_type=F32
        )

    def keep(n, r, current):
        current_ref(n, r)[...] = current
        if n < STEPS - 1:
            mid_only[R + r] = current

    def send_row(n, r):
        if n == STEPS - 1:
            out_start(n, r)
        elif r < HALF:
            @when(has_left)
            def _():
                to_left(n + 2, r).start()
        else:
            @when(has_right)
            def _():
                to_right(n + 2, r - HALF).start()

    def begin():
        twin_copy(0).wait_recv()
        own_sent(0)
        own_sent(1)
        for r in ORDER:
            if r == PARTS[part_of(r)][0]:
                far_wait(0, part_of(r))
            keep(0, r, (solved(0, r) - row_sum(r)).astype(BF16))
            send_row(0, r)
        for r in range(ROWS):
            out_start(0, r)

    def advance(n):
        products(n, mid_only)
        twin_copy(n).wait_recv()
        if n >= FINE:
            far_wait(n, 0)
        for r in ORDER:
            if n < FINE and r == PARTS[part_of(r)][0]:
                far_wait(n, part_of(r))
            base[r] = solved(n, r) - row_sum(r)
        if n == 2:
            halo_sent(2)

        def left():
            @when(has_left)
            def _():
                to_right(n + 1).wait_recv()

            rows(range(HALF))

        def right():
            @when(has_right)
            def _():
                to_left(n + 1).wait_recv()

            rows(range(HALF, ROWS))

        def rows(some):
            for r in some:
                current = base[r]
                for k, (row, c) in enumerate(PLACES):
                    if row == r:
                        current = current - jnp.dot(dense[k], xb[n + 1][c], preferred_element_type=F32)
                keep(n, r, current.astype(BF16))
                send_row(n, r)

        @when(far_right)
        def _():
            left()
            right()

        @when(jnp.logical_not(far_right))
        def _():
            right()
            left()

        if n < STEPS - 1:
            for r in range(ROWS):
                out_start(n, r)

    def share(n):
        if n > 0:
            twin_copy(n - 1).wait_send()
        for r in range(ROWS):
            stage[n, r] = row_sum(r).astype(BF16)
        twin_copy(n).start()

    def merged(n, r):
        return row_sum(r) + twin[n, r].astype(F32)

    def merge(n):
        twin_copy(n).wait_recv()
        if n > 0:
            mixed_sent(n - 1)

        @when(h == 5)
        def _():
            for r in ORDER:
                mixed[n, r] = merged(n, r).astype(BF16)
                tree_copy(n, r).start()

        for a, k, direct, via in ((3, 0, BY_THREE, BY_ONE), (7, 1, BY_ONE, BY_THREE)):
            @when(h == a)
            def _(k=k, direct=direct, via=via):
                for r in direct:
                    mixed[n, r] = merged(n, r).astype(BF16)
                    far_copy(n, k, r).start()
                for r in via:
                    tree_wait(n, via, r)
                    mixed[n, r] = (merged(n, r) + tree[n, r - via[0]].astype(F32)).astype(BF16)
                    far_copy(n, k, r).start()

    for i in range(3, len(loads)):
        load_wait(i)

    @when(march)
    def _():
        for i in range(2):
            march_load(i).wait()
        fold()

    own_wait()

    @when(march)
    def _():
        inside(2).start()
        inside(3).start()

    for n in range(STEPS):
        if n == 0:
            @when(even)
            def _():
                cross(2).wait_recv()
                own_sent(0)
                halo_start(2)

            products(0)

            @when(march)
            def _():
                begin()
        else:
            @when(even)
            def _(n=n):
                halo_wait(n + 1)

            @when(upper)
            def _(n=n):
                inside(n + 1).wait_recv()

            @when(march)
            def _(n=n):
                advance(n)
                if n == 1:
                    inside(4).start()

            @when(jnp.logical_not(march))
            def _(n=n):
                products(n)

        @when(odd == 0)
        def _(n=n):
            share(n)

        @when(gate)
        def _(n=n):
            merge(n)

        if n == 0:
            @when(even)
            def _():
                inside(2).start()
                inside(3).start()

            @when((odd == 0) & (h + 2 <= h_last))
            def _():
                cross(4).start()

            @when(even)
            def _():
                cross(3).wait_recv()
                halo_start(3)

        if n == 1:
            @when(even)
            def _():
                inside(4).start()
                cross(4).wait_recv()
                halo_sent(2)
                halo_start(4)

    @when(first)
    def _():
        for i in range(len(loads)):
            swap(i).wait_send()

    @when((h == 0) | gate)
    def _():
        own_sent(0)
        own_sent(1)

    @when(lower)
    def _():
        halo_sent(3)
        halo_sent(4)
        for j in (2, 3, 4):
            inside(j).wait_send()

    @when((odd == 1) & (h < h_last))
    def _():
        cross(2).wait_send()
        cross(3).wait_send()

    @when((odd == 0) & (h + 2 <= h_last))
    def _():
        cross(4).wait_send()

    @when(odd == 0)
    def _():
        twin_copy(STEPS - 1).wait_send()

    @when(gate)
    def _():
        mixed_sent(STEPS - 1)

    @when(march)
    def _():
        pltpu.make_async_copy(stage.at[0, pl.ds(0, STEPS)], out_ref, own_send).wait()
        remote(mixed.at[:, pl.ds(0, ROWS - 1)], mixed.at[:, pl.ds(0, ROWS - 1)], out_send, out_recv, at(hist=0)).wait_send()

    @when(jnp.logical_not(march))
    def _():
        remote(stage.at[0, pl.ds(0, STEPS)], out_ref, out_send, out_recv, at(hist=MARCH)).wait_recv()


def on_device(zblocks, slot_row, slot_offset, slot_delay, history, inverse, excite):
    _, cap, bs, _ = zblocks.shape
    columns = history.shape[2]
    slots = zblocks[0]
    past = history.reshape(history.shape[0], ROWS, bs, columns)
    inv = inverse.reshape(ROWS, bs, bs)
    exc = excite.reshape(STEPS, ROWS, bs, columns)
    operands = (slots, slot_row, slot_offset, slot_delay, past, inv, exc)
    any_spec = pl.BlockSpec(memory_space=pl.ANY)
    block = (bs, columns)
    dma = pltpu.SemaphoreType.DMA
    return pl.pallas_call(
        kernel,
        out_shape=pltpu.VMEM((STEPS, bs, columns), BF16),
        in_specs=[any_spec] * 7,
        out_specs=any_spec,
        scratch_shapes=[pltpu.VMEM((2, ROWS + 2 * R) + block, BF16)]
        + [pltpu.VMEM((ROWS + 2 * R,) + block, BF16) for _ in range(4)]
        + [
            pltpu.VMEM((ROWS,) + block, BF16),
            pltpu.VMEM((len(PLACES), bs, bs), BF16),
            pltpu.VMEM((cap, bs, bs), BF16),
            pltpu.VMEM((cap + 1,) + block, F32),
            pltpu.VMEM((STEPS, ROWS) + block, BF16),
            pltpu.VMEM((STEPS, ROWS) + block, BF16),
            pltpu.VMEM((STEPS, ROWS) + block, BF16),
            pltpu.VMEM((STEPS, len(BY_ONE)) + block, BF16),
            pltpu.VMEM((STEPS, 2, ROWS) + block, BF16),
            pltpu.VMEM((ROWS,) + block, F32),
            pltpu.VMEM((STEPS, ROWS) + block, BF16),
            pltpu.VMEM((ROWS, bs, bs), BF16),
            pltpu.SMEM((1, cap), jnp.int32),
            pltpu.SMEM((1, cap), jnp.int32),
            pltpu.SMEM((1, cap), jnp.int32),
            pltpu.SMEM((cap,), jnp.int32),
            pltpu.SMEM((cap,), jnp.int32),
            pltpu.SMEM((ROWS,), jnp.int32),
            pltpu.SMEM((cap,), jnp.int32),
            pltpu.SMEM((len(PLACES),), jnp.int32),
            pltpu.SemaphoreType.REGULAR,
            dma((7,)),
            dma((5,)),
            dma((2, 2)),
            dma((4, 2)),
            dma((3,)),
            dma((3,)),
            dma,
            dma((STEPS,)),
            dma,
            dma((FINE, 2, HALF)),
            dma((STEPS - FINE, 2)),
            dma((FINE, len(BY_ONE))),
            dma((STEPS - FINE,)),
            dma,
            dma,
            dma,
        ],
        compiler_params=pltpu.CompilerParams(
            collective_id=0, has_side_effects=True, vmem_limit_bytes=60 * 1024 * 1024
        ),
    )(*[pltpu.with_memory_space_constraint(v, pltpu.HBM) for v in operands])


def solution(mesh):
    return jax.shard_map(
        on_device,
        mesh=mesh,
        in_specs=(
            P("hist", "patch", None, None),
            P("hist", "patch"),
            P("hist", "patch"),
            P("hist", "patch"),
            P("hist", "patch", None),
            P("patch", None),
            P(None, "patch", None),
        ),
        out_specs=P(None, ("patch", "hist"), None),
        check_vma=False,
    )
```

```python
import jax
import jax.numpy as jnp
from jax import lax
from jax.experimental import pallas as pl
from jax.experimental.pallas import tpu as pltpu
from jax.sharding import PartitionSpec as P

R = 4
STEPS = 4
ROWS = 8
HALF = ROWS // 2
GROUP = 8
MARCH = 1
FINE = 2
BF16 = jnp.bfloat16
F32 = jnp.float32
PARTS = ((3, 7), (2, 6), (1, 5), (0, 4))
ORDER = tuple(r for part in PARTS for r in part)
LEFT = tuple((r, c) for r in range(HALF) for c in range(r, R))
RIGHT = tuple((r, c) for r in range(HALF, ROWS) for c in range(R + ROWS, r + 2 * R + 1))
PLACES = LEFT + RIGHT
WIDTH = ROWS + 2 * R
BY_ONE = (3, 2, 1, 0, 4)
BY_THREE = (7, 6, 5)


def kernel(
    z_hbm, row_hbm, off_hbm, dly_hbm, hist_hbm, inv_hbm, exc_hbm, out_ref,
    xa, xb2, xb3, xb4, mid_only, cur3, dense, zbuf, sums, stage, twin, mixed, tree, far, base, excv, invv,
    row_s, off_s, dly_s, col_s, prev_s, last_s, same_s, place_s,
    go_sem, load_sem, swap_send, halo_send, halo_recv, block_recv, shift_send, shift_recv,
    twin_send, twin_recv, red_send, far_first, far_recv, tree_first, tree_recv, out_send, own_send, out_recv,
):
    xb = (None, None, xb2, xb3, xb4)
    cap = z_hbm.shape[0]
    p = lax.axis_index("patch")
    h = lax.axis_index("hist")
    p_last = lax.axis_size("patch") - 1
    h_last = lax.axis_size("hist") - 1
    odd = h % 2
    first = h < 2
    later = h > 1
    lower = (h == MARCH) | (later & (odd == 0))
    upper = jnp.logical_not(lower)
    march = h == MARCH
    even = later & (odd == 0)
    gate = later & (odd == 1)
    has_left = p > 0
    has_right = p < p_last
    far_right = p % 8 == 7
    when = pl.when

    def at(patch=p, hist=h):
        return {"patch": patch, "hist": hist}

    barrier = pltpu.get_barrier_semaphore()

    def greet(where):
        pl.semaphore_signal(barrier, inc=1, device_id=where, device_id_type=pl.DeviceIdType.MESH)

    for side, q in ((has_left, p - 1), (has_right, p + 1)):
        @when(side & (h > 0))
        def _(q=q):
            greet(at(patch=q))

        @when(side & first)
        def _(q=q):
            greet(at(patch=q, hist=1 - h))

    lines = (
        (1, 2), (0, 2, 3, 4, 5, 6, 7), (0, 1, 3, 4), (1, 2, 4, 5),
        (1, 2, 3, 5, 6), (1, 3, 4, 6, 7), (1, 4, 5, 7), (1, 5, 6),
    )
    met = jnp.int32(0)
    for a, others in enumerate(lines):
        @when(h == a)
        def _(others=others):
            for b in others:
                greet(at(hist=b))

        met = jnp.where(h == a, len(others), met)
    sides = jnp.where(has_left, 1, 0) + jnp.where(has_right, 1, 0)
    met = met + sides * jnp.where(march, 2, 1)

    def remote(src, dst, ssem, rsem, where):
        return pltpu.make_async_remote_copy(
            src_ref=src, dst_ref=dst, send_sem=ssem, recv_sem=rsem,
            device_id=where, device_id_type=pl.DeviceIdType.MESH,
        )

    loads = (
        (row_hbm, row_s), (off_hbm, off_s), (dly_hbm, dly_s),
        (hist_hbm, xa.at[:, pl.ds(R, ROWS)]), (z_hbm, zbuf),
    )
    march_loads = ((inv_hbm, invv), (exc_hbm, excv))

    def load(i):
        return pltpu.make_async_copy(loads[i][0], loads[i][1], load_sem.at[i])

    def swap(i):
        return remote(loads[i][0], loads[i][1], swap_send.at[i], load_sem.at[i], at(hist=1 - h))

    def march_load(i):
        return pltpu.make_async_copy(march_loads[i][0], march_loads[i][1], load_sem.at[len(loads) + i])

    def load_wait(i):
        @when(first)
        def _():
            swap(i).wait_recv()

        @when(later)
        def _():
            load(i).wait()

    low, mid, high = pl.ds(0, R), pl.ds(R, ROWS), pl.ds(R + ROWS, R)

    partner = jnp.where(first, 1 - h, h)

    pieces = ((1, R // 2, R // 2), (0, 0, R), (1, 0, R // 2))

    def own_left(t):
        i, first_block, blocks = pieces[t]
        src = hist_hbm.at[i, pl.ds(first_block, blocks)]
        dst = xa.at[i, pl.ds(R + ROWS + first_block, blocks)]
        return remote(src, dst, halo_send.at[0, t // 2], halo_recv.at[0, 1], at(p - 1, partner))

    def own_right(t):
        i, first_block, blocks = pieces[t]
        src = hist_hbm.at[i, pl.ds(ROWS - R + first_block, blocks)]
        dst = xa.at[i, pl.ds(first_block, blocks)]
        return remote(src, dst, halo_send.at[1, t // 2], halo_recv.at[0, 0], at(p + 1, partner))

    def own_start():
        for t in (2, 0, 1):
            @when(has_left)
            def _(t=t):
                own_left(t).start()

            @when(has_right)
            def _(t=t):
                own_right(t).start()

    def own_sent(t):
        some = xb2.at[pl.ds(0, R // 2 if t == 1 else R + R // 2)]
        for side, present in enumerate((has_left, has_right)):
            @when(present)
            def _(side=side):
                remote(some, some, halo_send.at[side, t], halo_recv.at[0, 0], at()).wait_send()

    def own_wait():
        @when(has_left)
        def _():
            remote(hist_hbm.at[:, pl.ds(0, R)], xa.at[:, low], halo_send.at[0, 0], halo_recv.at[0, 0], at(p - 1)).wait_recv()

        @when(has_right)
        def _():
            remote(hist_hbm.at[:, pl.ds(0, R)], xa.at[:, high], halo_send.at[0, 0], halo_recv.at[0, 1], at(p + 1)).wait_recv()

    def to_left(j, q=None):
        src, dst = (xb[j].at[pl.ds(R, R)], xb[j].at[high]) if q is None else (xb[j].at[R + q], xb[j].at[R + ROWS + q])
        return remote(src, dst, halo_send.at[0, j % 2], halo_recv.at[j - 1, 1], at(p - 1))

    def to_right(j, q=None):
        src, dst = (xb[j].at[pl.ds(ROWS, R)], xb[j].at[low]) if q is None else (xb[j].at[ROWS + q], xb[j].at[q])
        rsem = halo_recv.at[j - 1, 0] if q is None else block_recv.at[j - 2, q]
        return remote(src, dst, halo_send.at[1, j % 2], rsem, at(p + 1))

    def halo_start(j):
        @when(has_left)
        def _():
            to_left(j).start()

        @when(has_right)
        def _():
            to_right(j).start()

    def halo_wait(j):
        @when(has_left)
        def _():
            to_right(j).wait_recv()

        @when(has_right)
        def _():
            to_left(j).wait_recv()

    def halo_sent(j):
        @when(has_left)
        def _():
            to_left(j).wait_send()

        @when(has_right)
        def _():
            to_right(j).wait_send()

    def cross(j):
        src, to = (hist_hbm.at[3 - j], h + 1) if j < 4 else (hist_hbm.at[1], h + 2)
        return remote(src, xb[j].at[mid], shift_send.at[j - 2], shift_recv.at[j - 2], at(hist=to))

    def inside(j):
        src = xa.at[3 - j] if j < 4 else xb2
        return remote(src, xb[j], shift_send.at[j - 2], shift_recv.at[j - 2], at(hist=h + 1 - 2 * odd))

    @when(later)
    def _():
        for i in range(len(loads)):
            load(i).start()

    @when(march)
    def _():
        for i in range(2):
            march_load(i).start()

    pl.semaphore_wait(barrier, met)

    @when(first | even)
    def _():
        own_start()

    @when((odd == 1) & (h < h_last))
    def _():
        cross(2).start()
        cross(3).start()

    @when(first)
    def _():
        for i in range(len(loads)):
            swap(i).start()

    @when(even)
    def _():
        own_sent(1)
        pl.semaphore_signal(go_sem, inc=1, device_id=at(hist=h + 1), device_id_type=pl.DeviceIdType.MESH)

    @when(gate)
    def _():
        pl.semaphore_wait(go_sem, 1)
        own_start()

    for edge, where in ((p == 0, low), (p == p_last, high)):
        @when(edge)
        def _(where=where):
            for i in range(2):
                xa[i, where] = jnp.zeros((R,) + xb2.shape[1:], BF16)

        @when(edge & lower)
        def _(where=where):
            for j in (2, 3, 4):
                xb[j][where] = jnp.zeros((R,) + xb2.shape[1:], BF16)

    sums[cap] = jnp.zeros(sums.shape[1:], F32)
    for i in range(3):
        load_wait(i)

    def note(s, last):
        row = row_s[0, s]
        col_s[s] = row + off_s[0, s]
        before = jnp.int32(cap)
        for r in range(ROWS):
            before = jnp.where(row == r, last[r], before)
        prev_s[s] = before
        return tuple(jnp.where(row == r, s, last[r]) for r in range(ROWS))

    last = lax.fori_loop(0, cap, note, (jnp.int32(cap),) * ROWS)
    for r in range(ROWS):
        last_s[r] = last[r]

    @when(march)
    def _():
        def note_place(s, seen):
            place = jnp.where(dly_s[0, s] == 0, row_s[0, s] * WIDTH + col_s[s], -1)
            before = jnp.int32(cap)
            for k, (r, c) in enumerate(PLACES):
                before = jnp.where(place == r * WIDTH + c, seen[k], before)
            same_s[s] = before
            return tuple(jnp.where(place == r * WIDTH + c, s, seen[k]) for k, (r, c) in enumerate(PLACES))

        seen = lax.fori_loop(0, cap, note_place, (jnp.int32(cap),) * len(PLACES))
        for k in range(len(PLACES)):
            place_s[k] = seen[k]
        mid_only[low] = jnp.zeros((R,) + xb2.shape[1:], BF16)
        mid_only[high] = jnp.zeros((R,) + xb2.shape[1:], BF16)

    def products(n, newest=None):
        for s in range(cap):
            col = col_s[s]
            delay = dly_s[0, s]
            if n == 0:
                x = xa[delay, col]
            else:
                new = xb[n + 1][col] if newest is None else newest[col]
                x = jnp.where(delay == 1, xa[0, col] if n == 1 else xb[n][col], new)
            sums[s] = sums[prev_s[s]] + jnp.dot(zbuf[s], x, preferred_element_type=F32)

    def row_sum(r):
        return sums[last_s[r]]

    def twin_copy(n):
        return remote(stage.at[n], twin.at[n], twin_send, twin_recv.at[n], at(hist=h + 1))

    def part_of(r):
        return [r in part for part in PARTS].index(True)

    def far_copy(n, k, r):
        rsem = far_first.at[n, k, part_of(r)] if n < FINE else far_recv.at[n - FINE, k]
        return remote(mixed.at[n, r], far.at[n, k, r], red_send, rsem, at(hist=MARCH))

    def tree_copy(n, r):
        to, i = (3, BY_ONE.index(r)) if r in BY_ONE else (7, BY_THREE.index(r))
        rsem = tree_first.at[n, i] if n < FINE else tree_recv.at[n - FINE]
        return remote(mixed.at[n, r], tree.at[n, i], red_send, rsem, at(hist=to))

    def mixed_sent(n):
        remote(mixed.at[n], mixed.at[n], red_send, red_send, at(hist=MARCH)).wait_send()

    def far_wait(n, part):
        for k in range(2):
            if n < FINE:
                src, dst, rsem = mixed.at[n, pl.ds(0, 2)], far.at[n, k, pl.ds(0, 2)], far_first.at[n, k, part]
            else:
                src, dst, rsem = mixed.at[n], far.at[n, k], far_recv.at[n - FINE, k]
            remote(src, dst, red_send, rsem, at()).wait_recv()

    def tree_wait(n, rows, r):
        if n < FINE:
            tree_copy(n, r).wait_recv()
        elif r == rows[0]:
            some = pl.ds(0, len(rows))
            remote(mixed.at[n, some], tree.at[n, some], red_send, tree_recv.at[n - FINE], at()).wait_recv()

    def current_ref(n, r):
        return cur3.at[r] if n == STEPS - 1 else xb[n + 2].at[R + r]

    def out_copy(n, r):
        return remote(current_ref(n, r), out_ref.at[n], out_send, out_recv, at(hist=r))

    def own_copy(n):
        return pltpu.make_async_copy(current_ref(n, MARCH), out_ref.at[n], own_send)

    def out_start(n, r):
        if r == MARCH:
            own_copy(n).start()
        else:
            out_copy(n, r).start()

    def fold():
        for slot in range(cap):
            folded = jnp.dot(invv[row_s[0, slot]], zbuf[slot], preferred_element_type=F32)
            zbuf[slot] = folded.astype(BF16)
            sums[slot] = sums[same_s[slot]] + folded
        for k in range(len(PLACES)):
            dense[k] = sums[place_s[k]].astype(BF16)

    def solved(n, r):
        total = twin[n, r].astype(F32) + far[n, 0, r].astype(F32) + far[n, 1, r].astype(F32)
        residual = excv[n, r].astype(F32) - total
        coarse = residual.astype(BF16)
        fine = (residual - coarse.astype(F32)).astype(BF16)
        return jnp.dot(invv[r], coarse, preferred_element_type=F32) + jnp.dot(
            invv[r], fine, preferred_element_type=F32
        )

    def keep(n, r, current):
        current_ref(n, r)[...] = current
        if n < STEPS - 1:
            mid_only[R + r] = current

    def send_row(n, r):
        if n == STEPS - 1:
            out_start(n, r)
        elif r < HALF:
            @when(has_left)
            def _():
                to_left(n + 2, r).start()
        else:
            @when(has_right)
            def _():
                to_right(n + 2, r - HALF).start()

    def begin():
        twin_copy(0).wait_recv()
        own_sent(0)
        own_sent(1)
        for r in ORDER:
            if r == PARTS[part_of(r)][0]:
                far_wait(0, part_of(r))
            keep(0, r, (solved(0, r) - row_sum(r)).astype(BF16))
            send_row(0, r)
        for r in range(ROWS):
            out_start(0, r)

    def advance(n):
        products(n, mid_only)
        twin_copy(n).wait_recv()
        if n >= FINE:
            far_wait(n, 0)
        for r in ORDER:
            if n < FINE and r == PARTS[part_of(r)][0]:
                far_wait(n, part_of(r))
            base[r] = solved(n, r) - row_sum(r)
        if n == 2:
            halo_sent(2)

        def finish(r):
            current = base[r]
            for k, (row, c) in enumerate(PLACES):
                if row == r:
                    current = current - jnp.dot(dense[k], xb[n + 1][c], preferred_element_type=F32)
            keep(n, r, current.astype(BF16))
            send_row(n, r)

        def left():
            for r in reversed(range(HALF)):
                @when(has_left)
                def _(r=r):
                    to_right(n + 1, r).wait_recv()

                finish(r)

        def right():
            @when(has_right)
            def _():
                to_left(n + 1).wait_recv()

            for r in reversed(range(HALF, ROWS)):
                finish(r)

        @when(far_right)
        def _():
            left()
            right()

        @when(jnp.logical_not(far_right))
        def _():
            right()
            left()

        if n < STEPS - 1:
            for r in range(ROWS):
                out_start(n, r)

    def share(n):
        if n > 0:
            twin_copy(n - 1).wait_send()
        for r in range(ROWS):
            stage[n, r] = row_sum(r).astype(BF16)
        twin_copy(n).start()

    def merged(n, r):
        return row_sum(r) + twin[n, r].astype(F32)

    def merge(n):
        twin_copy(n).wait_recv()
        if n > 0:
            mixed_sent(n - 1)

        @when(h == 5)
        def _():
            for r in ORDER:
                mixed[n, r] = merged(n, r).astype(BF16)
                tree_copy(n, r).start()

        for a, k, direct, via in ((3, 0, BY_THREE, BY_ONE), (7, 1, BY_ONE, BY_THREE)):
            @when(h == a)
            def _(k=k, direct=direct, via=via):
                for r in direct:
                    mixed[n, r] = merged(n, r).astype(BF16)
                    far_copy(n, k, r).start()
                for r in via:
                    tree_wait(n, via, r)
                    mixed[n, r] = (merged(n, r) + tree[n, via.index(r)].astype(F32)).astype(BF16)
                    far_copy(n, k, r).start()

    for i in range(3, len(loads)):
        load_wait(i)

    @when(march)
    def _():
        for i in range(2):
            march_load(i).wait()
        fold()

    own_wait()

    @when(march)
    def _():
        inside(2).start()
        inside(3).start()

    for n in range(STEPS):
        if n == 0:
            @when(even)
            def _():
                cross(2).wait_recv()
                own_sent(0)
                halo_start(2)

            products(0)

            @when(march)
            def _():
                begin()
        else:
            @when(even)
            def _(n=n):
                halo_wait(n + 1)

            @when(upper)
            def _(n=n):
                inside(n + 1).wait_recv()

            @when(march)
            def _(n=n):
                advance(n)
                if n == 1:
                    inside(4).start()

            @when(jnp.logical_not(march))
            def _(n=n):
                products(n)

        @when(odd == 0)
        def _(n=n):
            share(n)

        @when(gate)
        def _(n=n):
            merge(n)

        if n == 0:
            @when(even)
            def _():
                inside(2).start()
                inside(3).start()

            @when((odd == 0) & (h + 2 <= h_last))
            def _():
                cross(4).start()

            @when(even)
            def _():
                cross(3).wait_recv()
                halo_sent(2)
                halo_start(3)

        if n == 1:
            @when(even)
            def _():
                inside(4).start()
                cross(4).wait_recv()
                halo_start(4)

    @when(first)
    def _():
        for i in range(len(loads)):
            swap(i).wait_send()

    @when((h == 0) | gate)
    def _():
        own_sent(0)
        own_sent(1)

    @when(lower)
    def _():
        halo_sent(3)
        halo_sent(4)
        for j in (2, 3, 4):
            inside(j).wait_send()

    @when((odd == 1) & (h < h_last))
    def _():
        cross(2).wait_send()
        cross(3).wait_send()

    @when((odd == 0) & (h + 2 <= h_last))
    def _():
        cross(4).wait_send()

    @when(odd == 0)
    def _():
        twin_copy(STEPS - 1).wait_send()

    @when(gate)
    def _():
        mixed_sent(STEPS - 1)

    @when(march)
    def _():
        pltpu.make_async_copy(stage.at[0, pl.ds(0, STEPS)], out_ref, own_send).wait()
        remote(mixed.at[:, pl.ds(0, ROWS - 1)], mixed.at[:, pl.ds(0, ROWS - 1)], out_send, out_recv, at(hist=0)).wait_send()

    @when(jnp.logical_not(march))
    def _():
        remote(stage.at[0, pl.ds(0, STEPS)], out_ref, out_send, out_recv, at(hist=MARCH)).wait_recv()


def on_device(zblocks, slot_row, slot_offset, slot_delay, history, inverse, excite):
    _, cap, bs, _ = zblocks.shape
    columns = history.shape[2]
    slots = zblocks[0]
    past = history.reshape(history.shape[0], ROWS, bs, columns)
    inv = inverse.reshape(ROWS, bs, bs)
    exc = excite.reshape(STEPS, ROWS, bs, columns)
    operands = (slots, slot_row, slot_offset, slot_delay, past, inv, exc)
    any_spec = pl.BlockSpec(memory_space=pl.ANY)
    block = (bs, columns)
    dma = pltpu.SemaphoreType.DMA
    return pl.pallas_call(
        kernel,
        out_shape=pltpu.VMEM((STEPS, bs, columns), BF16),
        in_specs=[any_spec] * 7,
        out_specs=any_spec,
        scratch_shapes=[pltpu.VMEM((2, ROWS + 2 * R) + block, BF16)]
        + [pltpu.VMEM((ROWS + 2 * R,) + block, BF16) for _ in range(4)]
        + [
            pltpu.VMEM((ROWS,) + block, BF16),
            pltpu.VMEM((len(PLACES), bs, bs), BF16),
            pltpu.VMEM((cap, bs, bs), BF16),
            pltpu.VMEM((cap + 1,) + block, F32),
            pltpu.VMEM((STEPS, ROWS) + block, BF16),
            pltpu.VMEM((STEPS, ROWS) + block, BF16),
            pltpu.VMEM((STEPS, ROWS) + block, BF16),
            pltpu.VMEM((STEPS, len(BY_ONE)) + block, BF16),
            pltpu.VMEM((STEPS, 2, ROWS) + block, BF16),
            pltpu.VMEM((ROWS,) + block, F32),
            pltpu.VMEM((STEPS, ROWS) + block, BF16),
            pltpu.VMEM((ROWS, bs, bs), BF16),
            pltpu.SMEM((1, cap), jnp.int32),
            pltpu.SMEM((1, cap), jnp.int32),
            pltpu.SMEM((1, cap), jnp.int32),
            pltpu.SMEM((cap,), jnp.int32),
            pltpu.SMEM((cap,), jnp.int32),
            pltpu.SMEM((ROWS,), jnp.int32),
            pltpu.SMEM((cap,), jnp.int32),
            pltpu.SMEM((len(PLACES),), jnp.int32),
            pltpu.SemaphoreType.REGULAR,
            dma((7,)),
            dma((5,)),
            dma((2, 2)),
            dma((4, 2)),
            dma((STEPS - 1, R)),
            dma((3,)),
            dma((3,)),
            dma,
            dma((STEPS,)),
            dma,
            dma((FINE, 2, HALF)),
            dma((STEPS - FINE, 2)),
            dma((FINE, len(BY_ONE))),
            dma((STEPS - FINE,)),
            dma,
            dma,
            dma,
        ],
        compiler_params=pltpu.CompilerParams(
            collective_id=0, has_side_effects=True, vmem_limit_bytes=60 * 1024 * 1024
        ),
    )(*[pltpu.with_memory_space_constraint(v, pltpu.HBM) for v in operands])


def solution(mesh):
    return jax.shard_map(
        on_device,
        mesh=mesh,
        in_specs=(
            P("hist", "patch", None, None),
            P("hist", "patch"),
            P("hist", "patch"),
            P("hist", "patch"),
            P("hist", "patch", None),
            P("patch", None),
            P(None, "patch", None),
        ),
        out_specs=P(None, ("patch", "hist"), None),
        check_vma=False,
    )
```

```python
import jax
import jax.numpy as jnp
from jax import lax
from jax.experimental import pallas as pl
from jax.experimental.pallas import tpu as pltpu
from jax.sharding import PartitionSpec as P

R = 4
STEPS = 4
ROWS = 8
HALF = ROWS // 2
GROUP = 8
MARCH = 1
FINE = 2
BF16 = jnp.bfloat16
F32 = jnp.float32
PARTS = ((3, 7), (2, 6), (1, 5), (0, 4))
ORDER = tuple(r for part in PARTS for r in part)
LEFT = tuple((r, c) for r in range(HALF) for c in range(r, R))
RIGHT = tuple((r, c) for r in range(HALF, ROWS) for c in range(R + ROWS, r + 2 * R + 1))
PLACES = LEFT + RIGHT
WIDTH = ROWS + 2 * R
BY_ONE = (3, 2, 1, 0, 4)
BY_THREE = (7, 6, 5)


def kernel(
    z_hbm, row_hbm, off_hbm, dly_hbm, hist_hbm, inv_hbm, exc_hbm, out_ref,
    xa, xb2, xb3, xb4, mid_only, cur3, dense, zbuf, sums, stage, twin, mixed, tree, far, base, excv, invv,
    row_s, off_s, dly_s, col_s, prev_s, last_s, same_s, place_s,
    go_sem, back_sem, load_sem, swap_send, halo_send, halo_recv, block_recv, shift_send, shift_recv,
    twin_send, twin_recv, red_send, far_first, far_recv, tree_first, tree_recv, out_send, own_send, out_recv,
):
    xb = (None, None, xb2, xb3, xb4)
    cap = z_hbm.shape[0]
    p = lax.axis_index("patch")
    h = lax.axis_index("hist")
    p_last = lax.axis_size("patch") - 1
    h_last = lax.axis_size("hist") - 1
    odd = h % 2
    first = h < 2
    later = h > 1
    lower = (h == MARCH) | (later & (odd == 0))
    upper = jnp.logical_not(lower)
    march = h == MARCH
    even = later & (odd == 0)
    gate = later & (odd == 1)
    has_left = p > 0
    has_right = p < p_last
    far_right = p % 8 == 7
    when = pl.when

    def at(patch=p, hist=h):
        return {"patch": patch, "hist": hist}

    barrier = pltpu.get_barrier_semaphore()

    def greet(where):
        pl.semaphore_signal(barrier, inc=1, device_id=where, device_id_type=pl.DeviceIdType.MESH)

    for side, q in ((has_left, p - 1), (has_right, p + 1)):
        @when(side & (h > 0))
        def _(q=q):
            greet(at(patch=q))

        @when(side & first)
        def _(q=q):
            greet(at(patch=q, hist=1 - h))

    lines = (
        (1, 2), (0, 2, 3, 4, 5, 6, 7), (0, 1, 3, 4), (1, 2, 4, 5),
        (1, 2, 3, 5, 6), (1, 3, 4, 6, 7), (1, 4, 5, 7), (1, 5, 6),
    )
    met = jnp.int32(0)
    for a, others in enumerate(lines):
        @when(h == a)
        def _(others=others):
            for b in others:
                greet(at(hist=b))

        met = jnp.where(h == a, len(others), met)
    sides = jnp.where(has_left, 1, 0) + jnp.where(has_right, 1, 0)
    met = met + sides * jnp.where(march, 2, 1)

    def remote(src, dst, ssem, rsem, where):
        return pltpu.make_async_remote_copy(
            src_ref=src, dst_ref=dst, send_sem=ssem, recv_sem=rsem,
            device_id=where, device_id_type=pl.DeviceIdType.MESH,
        )

    loads = (
        (row_hbm, row_s), (off_hbm, off_s), (dly_hbm, dly_s),
        (hist_hbm, xa.at[:, pl.ds(R, ROWS)]), (z_hbm, zbuf),
    )
    march_loads = ((inv_hbm, invv), (exc_hbm, excv))

    def load(i):
        return pltpu.make_async_copy(loads[i][0], loads[i][1], load_sem.at[i])

    def swap(i):
        return remote(loads[i][0], loads[i][1], swap_send.at[i], load_sem.at[i], at(hist=1 - h))

    def march_load(i):
        return pltpu.make_async_copy(march_loads[i][0], march_loads[i][1], load_sem.at[len(loads) + i])

    def load_wait(i):
        @when(first)
        def _():
            swap(i).wait_recv()

        @when(later)
        def _():
            load(i).wait()

    low, mid, high = pl.ds(0, R), pl.ds(R, ROWS), pl.ds(R + ROWS, R)

    partner = jnp.where(first, 1 - h, h)

    pieces = ((1, R // 2, R // 2), (0, 0, R), (1, 0, R // 2))

    def own_left(t):
        i, first_block, blocks = pieces[t]
        src = hist_hbm.at[i, pl.ds(first_block, blocks)]
        dst = xa.at[i, pl.ds(R + ROWS + first_block, blocks)]
        return remote(src, dst, halo_send.at[0, t // 2], halo_recv.at[0, 1], at(p - 1, partner))

    def own_right(t):
        i, first_block, blocks = pieces[t]
        src = hist_hbm.at[i, pl.ds(ROWS - R + first_block, blocks)]
        dst = xa.at[i, pl.ds(first_block, blocks)]
        return remote(src, dst, halo_send.at[1, t // 2], halo_recv.at[0, 0], at(p + 1, partner))

    def own_start():
        for t in (2, 0, 1):
            @when(has_left)
            def _(t=t):
                own_left(t).start()

            @when(has_right)
            def _(t=t):
                own_right(t).start()

    def own_sent(t):
        some = xb2.at[pl.ds(0, R // 2 if t == 1 else R + R // 2)]
        for side, present in enumerate((has_left, has_right)):
            @when(present)
            def _(side=side):
                remote(some, some, halo_send.at[side, t], halo_recv.at[0, 0], at()).wait_send()

    def own_wait():
        @when(has_left)
        def _():
            remote(hist_hbm.at[:, pl.ds(0, R)], xa.at[:, low], halo_send.at[0, 0], halo_recv.at[0, 0], at(p - 1)).wait_recv()

        @when(has_right)
        def _():
            remote(hist_hbm.at[:, pl.ds(0, R)], xa.at[:, high], halo_send.at[0, 0], halo_recv.at[0, 1], at(p + 1)).wait_recv()

    def to_left(j, q=None):
        src, dst = (xb[j].at[pl.ds(R, R)], xb[j].at[high]) if q is None else (xb[j].at[R + q], xb[j].at[R + ROWS + q])
        return remote(src, dst, halo_send.at[0, j % 2], halo_recv.at[j - 1, 1], at(p - 1))

    def to_right(j, q=None):
        src, dst = (xb[j].at[pl.ds(ROWS, R)], xb[j].at[low]) if q is None else (xb[j].at[ROWS + q], xb[j].at[q])
        rsem = halo_recv.at[j - 1, 0] if q is None else block_recv.at[j - 2, q]
        return remote(src, dst, halo_send.at[1, j % 2], rsem, at(p + 1))

    def halo_start(j):
        @when(has_left)
        def _():
            to_left(j).start()

        @when(has_right)
        def _():
            to_right(j).start()

    def halo_wait(j):
        @when(has_left)
        def _():
            to_right(j).wait_recv()

        @when(has_right)
        def _():
            to_left(j).wait_recv()

    def halo_sent(j):
        @when(has_left)
        def _():
            to_left(j).wait_send()

        @when(has_right)
        def _():
            to_right(j).wait_send()

    def cross(j):
        src, to = (hist_hbm.at[3 - j], h + 1) if j < 4 else (hist_hbm.at[1], h + 2)
        return remote(src, xb[j].at[mid], shift_send.at[j - 2], shift_recv.at[j - 2], at(hist=to))

    def inside(j):
        src = xa.at[3 - j] if j < 4 else xb2
        return remote(src, xb[j], shift_send.at[j - 2], shift_recv.at[j - 2], at(hist=h + 1 - 2 * odd))

    @when(later)
    def _():
        for i in range(len(loads)):
            load(i).start()

    @when(march)
    def _():
        for i in range(2):
            march_load(i).start()

    pl.semaphore_wait(barrier, met)

    @when(first | even)
    def _():
        own_start()

    @when((odd == 1) & (h < h_last))
    def _():
        cross(2).start()

    @when(first)
    def _():
        for i in range(len(loads)):
            swap(i).start()

    @when(even)
    def _():
        own_sent(1)
        pl.semaphore_signal(go_sem, inc=1, device_id=at(hist=h + 1), device_id_type=pl.DeviceIdType.MESH)

    @when(gate)
    def _():
        pl.semaphore_wait(go_sem, 1)
        own_start()

    for edge, where in ((p == 0, low), (p == p_last, high)):
        @when(edge)
        def _(where=where):
            for i in range(2):
                xa[i, where] = jnp.zeros((R,) + xb2.shape[1:], BF16)

        @when(edge & lower)
        def _(where=where):
            for j in (2, 3, 4):
                xb[j][where] = jnp.zeros((R,) + xb2.shape[1:], BF16)

    sums[cap] = jnp.zeros(sums.shape[1:], F32)
    for i in range(3):
        load_wait(i)

    def note(s, last):
        row = row_s[0, s]
        col_s[s] = row + off_s[0, s]
        before = jnp.int32(cap)
        for r in range(ROWS):
            before = jnp.where(row == r, last[r], before)
        prev_s[s] = before
        return tuple(jnp.where(row == r, s, last[r]) for r in range(ROWS))

    last = lax.fori_loop(0, cap, note, (jnp.int32(cap),) * ROWS)
    for r in range(ROWS):
        last_s[r] = last[r]

    @when((odd == 1) & (h < h_last))
    def _():
        cross(2).wait_send()
        cross(3).start()

    @when(gate)
    def _():
        own_sent(1)
        own_sent(0)
        pl.semaphore_signal(back_sem, inc=1, device_id=at(hist=h - 1), device_id_type=pl.DeviceIdType.MESH)

    @when(march)
    def _():
        def note_place(s, seen):
            place = jnp.where(dly_s[0, s] == 0, row_s[0, s] * WIDTH + col_s[s], -1)
            before = jnp.int32(cap)
            for k, (r, c) in enumerate(PLACES):
                before = jnp.where(place == r * WIDTH + c, seen[k], before)
            same_s[s] = before
            return tuple(jnp.where(place == r * WIDTH + c, s, seen[k]) for k, (r, c) in enumerate(PLACES))

        seen = lax.fori_loop(0, cap, note_place, (jnp.int32(cap),) * len(PLACES))
        for k in range(len(PLACES)):
            place_s[k] = seen[k]
        mid_only[low] = jnp.zeros((R,) + xb2.shape[1:], BF16)
        mid_only[high] = jnp.zeros((R,) + xb2.shape[1:], BF16)

    def products(n, newest=None):
        for s in range(cap):
            col = col_s[s]
            delay = dly_s[0, s]
            if n == 0:
                x = xa[delay, col]
            else:
                new = xb[n + 1][col] if newest is None else newest[col]
                x = jnp.where(delay == 1, xa[0, col] if n == 1 else xb[n][col], new)
            sums[s] = sums[prev_s[s]] + jnp.dot(zbuf[s], x, preferred_element_type=F32)

    def row_sum(r):
        return sums[last_s[r]]

    def twin_copy(n):
        return remote(stage.at[n], twin.at[n], twin_send, twin_recv.at[n], at(hist=h + 1))

    def part_of(r):
        return [r in part for part in PARTS].index(True)

    def far_copy(n, k, r):
        rsem = far_first.at[n, k, part_of(r)] if n < FINE else far_recv.at[n - FINE, k]
        return remote(mixed.at[n, r], far.at[n, k, r], red_send, rsem, at(hist=MARCH))

    def tree_copy(n, r):
        to, i = (3, BY_ONE.index(r)) if r in BY_ONE else (7, BY_THREE.index(r))
        rsem = tree_first.at[n, i] if n < FINE else tree_recv.at[n - FINE]
        return remote(mixed.at[n, r], tree.at[n, i], red_send, rsem, at(hist=to))

    def mixed_sent(n):
        remote(mixed.at[n], mixed.at[n], red_send, red_send, at(hist=MARCH)).wait_send()

    def far_wait(n, part):
        for k in range(2):
            if n < FINE:
                src, dst, rsem = mixed.at[n, pl.ds(0, 2)], far.at[n, k, pl.ds(0, 2)], far_first.at[n, k, part]
            else:
                src, dst, rsem = mixed.at[n], far.at[n, k], far_recv.at[n - FINE, k]
            remote(src, dst, red_send, rsem, at()).wait_recv()

    def tree_wait(n, rows, r):
        if n < FINE:
            tree_copy(n, r).wait_recv()
        elif r == rows[0]:
            some = pl.ds(0, len(rows))
            remote(mixed.at[n, some], tree.at[n, some], red_send, tree_recv.at[n - FINE], at()).wait_recv()

    def current_ref(n, r):
        return cur3.at[r] if n == STEPS - 1 else xb[n + 2].at[R + r]

    def out_copy(n, r):
        return remote(current_ref(n, r), out_ref.at[n], out_send, out_recv, at(hist=r))

    def own_copy(n):
        return pltpu.make_async_copy(current_ref(n, MARCH), out_ref.at[n], own_send)

    def out_start(n, r):
        if r == MARCH:
            own_copy(n).start()
        else:
            out_copy(n, r).start()

    def fold():
        for slot in range(cap):
            folded = jnp.dot(invv[row_s[0, slot]], zbuf[slot], preferred_element_type=F32)
            zbuf[slot] = folded.astype(BF16)
            sums[slot] = sums[same_s[slot]] + folded
        for k in range(len(PLACES)):
            dense[k] = sums[place_s[k]].astype(BF16)

    def solved(n, r):
        total = twin[n, r].astype(F32) + far[n, 0, r].astype(F32) + far[n, 1, r].astype(F32)
        residual = excv[n, r].astype(F32) - total
        coarse = residual.astype(BF16)
        fine = (residual - coarse.astype(F32)).astype(BF16)
        return jnp.dot(invv[r], coarse, preferred_element_type=F32) + jnp.dot(
            invv[r], fine, preferred_element_type=F32
        )

    def keep(n, r, current):
        current_ref(n, r)[...] = current
        if n < STEPS - 1:
            mid_only[R + r] = current

    def send_row(n, r):
        if n == STEPS - 1:
            out_start(n, r)
        elif r < HALF:
            @when(has_left)
            def _():
                to_left(n + 2, r).start()
        else:
            @when(has_right)
            def _():
                to_right(n + 2, r - HALF).start()

    def begin():
        twin_copy(0).wait_recv()
        own_sent(0)
        own_sent(1)
        for r in ORDER:
            if r == PARTS[part_of(r)][0]:
                far_wait(0, part_of(r))
            keep(0, r, (solved(0, r) - row_sum(r)).astype(BF16))
            send_row(0, r)
        for r in range(ROWS):
            out_start(0, r)

    def advance(n):
        products(n, mid_only)
        twin_copy(n).wait_recv()
        if n >= FINE:
            far_wait(n, 0)
        for r in ORDER:
            if n < FINE and r == PARTS[part_of(r)][0]:
                far_wait(n, part_of(r))
            base[r] = solved(n, r) - row_sum(r)
        if n == 2:
            halo_sent(2)

        def finish(r):
            current = base[r]
            for k, (row, c) in enumerate(PLACES):
                if row == r:
                    current = current - jnp.dot(dense[k], xb[n + 1][c], preferred_element_type=F32)
            keep(n, r, current.astype(BF16))
            send_row(n, r)

        def left():
            for r in reversed(range(HALF)):
                @when(has_left)
                def _(r=r):
                    to_right(n + 1, r).wait_recv()

                finish(r)

        def right():
            @when(has_right)
            def _():
                to_left(n + 1).wait_recv()

            for r in reversed(range(HALF, ROWS)):
                finish(r)

        @when(far_right)
        def _():
            left()
            right()

        @when(jnp.logical_not(far_right))
        def _():
            right()
            left()

        if n < STEPS - 1:
            for r in range(ROWS):
                out_start(n, r)

    def share(n):
        if n > 0:
            twin_copy(n - 1).wait_send()
        for r in range(ROWS):
            stage[n, r] = row_sum(r).astype(BF16)
        twin_copy(n).start()

    def merged(n, r):
        return row_sum(r) + twin[n, r].astype(F32)

    def merge(n):
        twin_copy(n).wait_recv()
        if n > 0:
            mixed_sent(n - 1)

        @when(h == 5)
        def _():
            for r in ORDER:
                mixed[n, r] = merged(n, r).astype(BF16)
                tree_copy(n, r).start()

        for a, k, direct, via in ((3, 0, BY_THREE, BY_ONE), (7, 1, BY_ONE, BY_THREE)):
            @when(h == a)
            def _(k=k, direct=direct, via=via):
                for r in direct:
                    mixed[n, r] = merged(n, r).astype(BF16)
                    far_copy(n, k, r).start()
                for r in via:
                    tree_wait(n, via, r)
                    mixed[n, r] = (merged(n, r) + tree[n, via.index(r)].astype(F32)).astype(BF16)
                    far_copy(n, k, r).start()

    for i in range(3, len(loads)):
        load_wait(i)

    @when(march)
    def _():
        for i in range(2):
            march_load(i).wait()
        fold()

    @when(even)
    def _():
        pl.semaphore_wait(back_sem, 1)
        cross(2).wait_recv()
        own_sent(0)
        halo_start(2)

    own_wait()

    @when(march)
    def _():
        inside(2).start()
        inside(3).start()

    for n in range(STEPS):
        if n == 0:
            products(0)

            @when(march)
            def _():
                begin()
        else:
            @when(even)
            def _(n=n):
                halo_wait(n + 1)

            @when(upper)
            def _(n=n):
                inside(n + 1).wait_recv()

            @when(march)
            def _(n=n):
                advance(n)
                if n == 1:
                    inside(4).start()

            @when(jnp.logical_not(march))
            def _(n=n):
                products(n)

        @when(odd == 0)
        def _(n=n):
            share(n)

        @when(gate)
        def _(n=n):
            merge(n)

        if n == 0:
            @when(even)
            def _():
                inside(2).start()
                inside(3).start()

            @when((odd == 0) & (h + 2 <= h_last))
            def _():
                cross(4).start()

            @when(even)
            def _():
                cross(3).wait_recv()
                halo_sent(2)
                halo_start(3)

        if n == 1:
            @when(even)
            def _():
                inside(4).start()
                cross(4).wait_recv()
                halo_start(4)

    @when(first)
    def _():
        for i in range(len(loads)):
            swap(i).wait_send()

    @when(h == 0)
    def _():
        own_sent(0)
        own_sent(1)

    @when(lower)
    def _():
        halo_sent(3)
        halo_sent(4)
        for j in (2, 3, 4):
            inside(j).wait_send()

    @when((odd == 1) & (h < h_last))
    def _():
        cross(3).wait_send()

    @when((odd == 0) & (h + 2 <= h_last))
    def _():
        cross(4).wait_send()

    @when(odd == 0)
    def _():
        twin_copy(STEPS - 1).wait_send()

    @when(gate)
    def _():
        mixed_sent(STEPS - 1)

    @when(march)
    def _():
        pltpu.make_async_copy(stage.at[0, pl.ds(0, STEPS)], out_ref, own_send).wait()
        remote(mixed.at[:, pl.ds(0, ROWS - 1)], mixed.at[:, pl.ds(0, ROWS - 1)], out_send, out_recv, at(hist=0)).wait_send()

    @when(jnp.logical_not(march))
    def _():
        remote(stage.at[0, pl.ds(0, STEPS)], out_ref, out_send, out_recv, at(hist=MARCH)).wait_recv()


def on_device(zblocks, slot_row, slot_offset, slot_delay, history, inverse, excite):
    _, cap, bs, _ = zblocks.shape
    columns = history.shape[2]
    slots = zblocks[0]
    past = history.reshape(history.shape[0], ROWS, bs, columns)
    inv = inverse.reshape(ROWS, bs, bs)
    exc = excite.reshape(STEPS, ROWS, bs, columns)
    operands = (slots, slot_row, slot_offset, slot_delay, past, inv, exc)
    any_spec = pl.BlockSpec(memory_space=pl.ANY)
    block = (bs, columns)
    dma = pltpu.SemaphoreType.DMA
    return pl.pallas_call(
        kernel,
        out_shape=pltpu.VMEM((STEPS, bs, columns), BF16),
        in_specs=[any_spec] * 7,
        out_specs=any_spec,
        scratch_shapes=[pltpu.VMEM((2, ROWS + 2 * R) + block, BF16)]
        + [pltpu.VMEM((ROWS + 2 * R,) + block, BF16) for _ in range(4)]
        + [
            pltpu.VMEM((ROWS,) + block, BF16),
            pltpu.VMEM((len(PLACES), bs, bs), BF16),
            pltpu.VMEM((cap, bs, bs), BF16),
            pltpu.VMEM((cap + 1,) + block, F32),
            pltpu.VMEM((STEPS, ROWS) + block, BF16),
            pltpu.VMEM((STEPS, ROWS) + block, BF16),
            pltpu.VMEM((STEPS, ROWS) + block, BF16),
            pltpu.VMEM((STEPS, len(BY_ONE)) + block, BF16),
            pltpu.VMEM((STEPS, 2, ROWS) + block, BF16),
            pltpu.VMEM((ROWS,) + block, F32),
            pltpu.VMEM((STEPS, ROWS) + block, BF16),
            pltpu.VMEM((ROWS, bs, bs), BF16),
            pltpu.SMEM((1, cap), jnp.int32),
            pltpu.SMEM((1, cap), jnp.int32),
            pltpu.SMEM((1, cap), jnp.int32),
            pltpu.SMEM((cap,), jnp.int32),
            pltpu.SMEM((cap,), jnp.int32),
            pltpu.SMEM((ROWS,), jnp.int32),
            pltpu.SMEM((cap,), jnp.int32),
            pltpu.SMEM((len(PLACES),), jnp.int32),
            pltpu.SemaphoreType.REGULAR,
            pltpu.SemaphoreType.REGULAR,
            dma((7,)),
            dma((5,)),
            dma((2, 2)),
            dma((4, 2)),
            dma((STEPS - 1, R)),
            dma((3,)),
            dma((3,)),
            dma,
            dma((STEPS,)),
            dma,
            dma((FINE, 2, HALF)),
            dma((STEPS - FINE, 2)),
            dma((FINE, len(BY_ONE))),
            dma((STEPS - FINE,)),
            dma,
            dma,
            dma,
        ],
        compiler_params=pltpu.CompilerParams(
            collective_id=0, has_side_effects=True, vmem_limit_bytes=60 * 1024 * 1024
        ),
    )(*[pltpu.with_memory_space_constraint(v, pltpu.HBM) for v in operands])


def solution(mesh):
    return jax.shard_map(
        on_device,
        mesh=mesh,
        in_specs=(
            P("hist", "patch", None, None),
            P("hist", "patch"),
            P("hist", "patch"),
            P("hist", "patch"),
            P("hist", "patch", None),
            P("patch", None),
            P(None, "patch", None),
        ),
        out_specs=P(None, ("patch", "hist"), None),
        check_vma=False,
    )
```

```python
import jax
import jax.numpy as jnp
from jax import lax
from jax.experimental import pallas as pl
from jax.experimental.pallas import tpu as pltpu
from jax.sharding import PartitionSpec as P

R = 4
STEPS = 4
ROWS = 8
HALF = ROWS // 2
GROUP = 8
MARCH = 1
FINE = 2
BF16 = jnp.bfloat16
F32 = jnp.float32
PARTS = ((3, 7), (2, 6), (1, 5), (0, 4))
ORDER = tuple(r for part in PARTS for r in part)
LEFT = tuple((r, c) for r in range(HALF) for c in range(r, R))
RIGHT = tuple((r, c) for r in range(HALF, ROWS) for c in range(R + ROWS, r + 2 * R + 1))
PLACES = LEFT + RIGHT
WIDTH = ROWS + 2 * R
BY_ONE = (3, 2, 1, 0, 4)
BY_THREE = (7, 6, 5)


def kernel(
    z_hbm, row_hbm, off_hbm, dly_hbm, hist_hbm, inv_hbm, exc_hbm, out_ref,
    xa, xb2, xb3, xb4, mid_only, cur3, dense, zbuf, sums, stage, twin, mixed, tree, far, base, excv, invv,
    row_s, off_s, dly_s, col_s, prev_s, last_s, same_s, place_s,
    go_sem, back_sem, load_sem, swap_send, halo_send, halo_recv, block_recv, shift_send, shift_recv,
    twin_send, twin_recv, red_send, far_first, far_recv, tree_first, tree_recv, out_send, own_send, out_recv,
):
    xb = (None, None, xb2, xb3, xb4)
    cap = z_hbm.shape[0]
    p = lax.axis_index("patch")
    h = lax.axis_index("hist")
    p_last = lax.axis_size("patch") - 1
    h_last = lax.axis_size("hist") - 1
    odd = h % 2
    first = h < 2
    later = h > 1
    lower = (h == MARCH) | (later & (odd == 0))
    upper = jnp.logical_not(lower)
    march = h == MARCH
    even = later & (odd == 0)
    gate = later & (odd == 1)
    has_left = p > 0
    has_right = p < p_last
    far_right = p % 8 == 7
    when = pl.when

    def at(patch=p, hist=h):
        return {"patch": patch, "hist": hist}

    barrier = pltpu.get_barrier_semaphore()

    def greet(where):
        pl.semaphore_signal(barrier, inc=1, device_id=where, device_id_type=pl.DeviceIdType.MESH)

    for side, q in ((has_right, p + 1), (has_left, p - 1)):
        @when(side & (h > 0))
        def _(q=q):
            greet(at(patch=q))

        @when(side & first)
        def _(q=q):
            greet(at(patch=q, hist=1 - h))

    lines = (
        (1, 2), (0, 2, 3, 4, 5, 6, 7), (0, 1, 3, 4), (1, 2, 4, 5),
        (1, 2, 3, 5, 6), (1, 3, 4, 6, 7), (1, 4, 5, 7), (1, 5, 6),
    )
    met = jnp.int32(0)
    for a, others in enumerate(lines):
        @when(h == a)
        def _(others=others):
            for b in others:
                greet(at(hist=b))

        met = jnp.where(h == a, len(others), met)
    sides = jnp.where(has_left, 1, 0) + jnp.where(has_right, 1, 0)
    met = met + sides * jnp.where(march, 2, 1)

    def remote(src, dst, ssem, rsem, where):
        return pltpu.make_async_remote_copy(
            src_ref=src, dst_ref=dst, send_sem=ssem, recv_sem=rsem,
            device_id=where, device_id_type=pl.DeviceIdType.MESH,
        )

    loads = (
        (row_hbm, row_s), (off_hbm, off_s), (dly_hbm, dly_s),
        (hist_hbm, xa.at[:, pl.ds(R, ROWS)]), (z_hbm, zbuf),
    )
    march_loads = ((inv_hbm, invv), (exc_hbm, excv))

    def load(i):
        return pltpu.make_async_copy(loads[i][0], loads[i][1], load_sem.at[i])

    def swap(i):
        return remote(loads[i][0], loads[i][1], swap_send.at[i], load_sem.at[i], at(hist=1 - h))

    def march_load(i):
        return pltpu.make_async_copy(march_loads[i][0], march_loads[i][1], load_sem.at[len(loads) + i])

    def load_wait(i):
        @when(first)
        def _():
            swap(i).wait_recv()

        @when(later)
        def _():
            load(i).wait()

    low, mid, high = pl.ds(0, R), pl.ds(R, ROWS), pl.ds(R + ROWS, R)

    partner = jnp.where(first, 1 - h, h)

    pieces = ((1, R // 2, R // 2), (0, 0, R), (1, 0, R // 2))

    def own_left(t):
        i, first_block, blocks = pieces[t]
        src = hist_hbm.at[i, pl.ds(first_block, blocks)]
        dst = xa.at[i, pl.ds(R + ROWS + first_block, blocks)]
        return remote(src, dst, halo_send.at[0, t // 2], halo_recv.at[0, 1], at(p - 1, partner))

    def own_right(t):
        i, first_block, blocks = pieces[t]
        src = hist_hbm.at[i, pl.ds(ROWS - R + first_block, blocks)]
        dst = xa.at[i, pl.ds(first_block, blocks)]
        return remote(src, dst, halo_send.at[1, t // 2], halo_recv.at[0, 0], at(p + 1, partner))

    def own_start():
        for t in (2, 0, 1):
            @when(has_left)
            def _(t=t):
                own_left(t).start()

            @when(has_right)
            def _(t=t):
                own_right(t).start()

    def own_sent(t):
        some = xb2.at[pl.ds(0, R // 2 if t == 1 else R + R // 2)]
        for side, present in enumerate((has_left, has_right)):
            @when(present)
            def _(side=side):
                remote(some, some, halo_send.at[side, t], halo_recv.at[0, 0], at()).wait_send()

    def own_wait():
        @when(has_left)
        def _():
            remote(hist_hbm.at[:, pl.ds(0, R)], xa.at[:, low], halo_send.at[0, 0], halo_recv.at[0, 0], at(p - 1)).wait_recv()

        @when(has_right)
        def _():
            remote(hist_hbm.at[:, pl.ds(0, R)], xa.at[:, high], halo_send.at[0, 0], halo_recv.at[0, 1], at(p + 1)).wait_recv()

    def to_left(j, q=None):
        src, dst = (xb[j].at[pl.ds(R, R)], xb[j].at[high]) if q is None else (xb[j].at[R + q], xb[j].at[R + ROWS + q])
        return remote(src, dst, halo_send.at[0, j % 2], halo_recv.at[j - 1, 1], at(p - 1))

    def to_right(j, q=None):
        src, dst = (xb[j].at[pl.ds(ROWS, R)], xb[j].at[low]) if q is None else (xb[j].at[ROWS + q], xb[j].at[q])
        rsem = halo_recv.at[j - 1, 0] if q is None else block_recv.at[j - 2, q]
        return remote(src, dst, halo_send.at[1, j % 2], rsem, at(p + 1))

    def halo_start(j):
        @when(has_left)
        def _():
            to_left(j).start()

        @when(has_right)
        def _():
            to_right(j).start()

    def halo_wait(j):
        @when(has_left)
        def _():
            to_right(j).wait_recv()

        @when(has_right)
        def _():
            to_left(j).wait_recv()

    def halo_sent(j):
        @when(has_left)
        def _():
            to_left(j).wait_send()

        @when(has_right)
        def _():
            to_right(j).wait_send()

    def cross(j):
        src, to = (hist_hbm.at[3 - j], h + 1) if j < 4 else (hist_hbm.at[1], h + 2)
        return remote(src, xb[j].at[mid], shift_send.at[j - 2], shift_recv.at[j - 2], at(hist=to))

    def inside(j):
        src = xa.at[3 - j] if j < 4 else xb2
        return remote(src, xb[j], shift_send.at[j - 2], shift_recv.at[j - 2], at(hist=h + 1 - 2 * odd))

    @when(later)
    def _():
        for i in range(len(loads)):
            load(i).start()

    @when(march)
    def _():
        for i in range(2):
            march_load(i).start()

    pl.semaphore_wait(barrier, met)

    @when(first | even)
    def _():
        own_start()

    @when((odd == 1) & (h < h_last))
    def _():
        cross(2).start()

    @when(first)
    def _():
        for i in range(len(loads)):
            swap(i).start()

    @when(even)
    def _():
        own_sent(1)
        pl.semaphore_signal(go_sem, inc=1, device_id=at(hist=h + 1), device_id_type=pl.DeviceIdType.MESH)

    @when(gate)
    def _():
        pl.semaphore_wait(go_sem, 1)
        own_start()

    for edge, where in ((p == 0, low), (p == p_last, high)):
        @when(edge)
        def _(where=where):
            for i in range(2):
                xa[i, where] = jnp.zeros((R,) + xb2.shape[1:], BF16)

        @when(edge & lower)
        def _(where=where):
            for j in (2, 3, 4):
                xb[j][where] = jnp.zeros((R,) + xb2.shape[1:], BF16)

    sums[cap] = jnp.zeros(sums.shape[1:], F32)
    for i in range(3):
        load_wait(i)

    def note(s, last):
        row = row_s[0, s]
        col_s[s] = row + off_s[0, s]
        before = jnp.int32(cap)
        for r in range(ROWS):
            before = jnp.where(row == r, last[r], before)
        prev_s[s] = before
        return tuple(jnp.where(row == r, s, last[r]) for r in range(ROWS))

    last = lax.fori_loop(0, cap, note, (jnp.int32(cap),) * ROWS)
    for r in range(ROWS):
        last_s[r] = last[r]

    @when((odd == 1) & (h < h_last))
    def _():
        cross(2).wait_send()
        cross(3).start()

    @when(gate)
    def _():
        own_sent(1)
        own_sent(0)
        pl.semaphore_signal(back_sem, inc=1, device_id=at(hist=h - 1), device_id_type=pl.DeviceIdType.MESH)

    @when(march)
    def _():
        def note_place(s, seen):
            place = jnp.where(dly_s[0, s] == 0, row_s[0, s] * WIDTH + col_s[s], -1)
            before = jnp.int32(cap)
            for k, (r, c) in enumerate(PLACES):
                before = jnp.where(place == r * WIDTH + c, seen[k], before)
            same_s[s] = before
            return tuple(jnp.where(place == r * WIDTH + c, s, seen[k]) for k, (r, c) in enumerate(PLACES))

        seen = lax.fori_loop(0, cap, note_place, (jnp.int32(cap),) * len(PLACES))
        for k in range(len(PLACES)):
            place_s[k] = seen[k]
        mid_only[low] = jnp.zeros((R,) + xb2.shape[1:], BF16)
        mid_only[high] = jnp.zeros((R,) + xb2.shape[1:], BF16)

    def products(n, newest=None):
        for s in range(cap):
            col = col_s[s]
            delay = dly_s[0, s]
            if n == 0:
                x = xa[delay, col]
            else:
                new = xb[n + 1][col] if newest is None else newest[col]
                x = jnp.where(delay == 1, xa[0, col] if n == 1 else xb[n][col], new)
            sums[s] = sums[prev_s[s]] + jnp.dot(zbuf[s], x, preferred_element_type=F32)

    def row_sum(r):
        return sums[last_s[r]]

    def twin_copy(n, c):
        some = pl.ds(HALF * c, HALF)
        return remote(stage.at[n, some], twin.at[n, some], twin_send, twin_recv.at[n, c], at(hist=h + 1))

    def twin_sent(n):
        remote(stage.at[n], stage.at[n], twin_send, twin_send, at()).wait_send()

    def twin_row(n, r):
        return twin[n, ORDER.index(r)].astype(F32)

    def part_of(r):
        return [r in part for part in PARTS].index(True)

    def far_copy(n, k, r):
        rsem = far_first.at[n, k, part_of(r)] if n < FINE else far_recv.at[n - FINE, k]
        return remote(mixed.at[n, r], far.at[n, k, r], red_send, rsem, at(hist=MARCH))

    def tree_copy(n, r):
        to, i = (3, BY_ONE.index(r)) if r in BY_ONE else (7, BY_THREE.index(r))
        rsem = tree_first.at[n, i] if n < FINE else tree_recv.at[n - FINE]
        return remote(mixed.at[n, r], tree.at[n, i], red_send, rsem, at(hist=to))

    def mixed_sent(n):
        remote(mixed.at[n], mixed.at[n], red_send, red_send, at(hist=MARCH)).wait_send()

    def far_wait(n, part):
        for k in range(2):
            if n < FINE:
                src, dst, rsem = mixed.at[n, pl.ds(0, 2)], far.at[n, k, pl.ds(0, 2)], far_first.at[n, k, part]
            else:
                src, dst, rsem = mixed.at[n], far.at[n, k], far_recv.at[n - FINE, k]
            remote(src, dst, red_send, rsem, at()).wait_recv()

    def tree_wait(n, rows, r):
        if n < FINE:
            tree_copy(n, r).wait_recv()
        elif r == rows[0]:
            some = pl.ds(0, len(rows))
            remote(mixed.at[n, some], tree.at[n, some], red_send, tree_recv.at[n - FINE], at()).wait_recv()

    def current_ref(n, r):
        return cur3.at[r] if n == STEPS - 1 else xb[n + 2].at[R + r]

    def out_copy(n, r):
        return remote(current_ref(n, r), out_ref.at[n], out_send, out_recv, at(hist=r))

    def own_copy(n):
        return pltpu.make_async_copy(current_ref(n, MARCH), out_ref.at[n], own_send)

    def out_start(n, r):
        if r == MARCH:
            own_copy(n).start()
        else:
            out_copy(n, r).start()

    def fold():
        for slot in range(cap):
            folded = jnp.dot(invv[row_s[0, slot]], zbuf[slot], preferred_element_type=F32)
            zbuf[slot] = folded.astype(BF16)
            sums[slot] = sums[same_s[slot]] + folded
        for k in range(len(PLACES)):
            dense[k] = sums[place_s[k]].astype(BF16)

    def solved(n, r):
        total = twin_row(n, r) + far[n, 0, r].astype(F32) + far[n, 1, r].astype(F32)
        residual = excv[n, r].astype(F32) - total
        coarse = residual.astype(BF16)
        fine = (residual - coarse.astype(F32)).astype(BF16)
        return jnp.dot(invv[r], coarse, preferred_element_type=F32) + jnp.dot(
            invv[r], fine, preferred_element_type=F32
        )

    def keep(n, r, current):
        current_ref(n, r)[...] = current
        if n < STEPS - 1:
            mid_only[R + r] = current

    def send_row(n, r):
        if n == STEPS - 1:
            out_start(n, r)
        elif r < HALF:
            @when(has_left)
            def _():
                to_left(n + 2, r).start()
        else:
            @when(has_right)
            def _():
                to_right(n + 2, r - HALF).start()

    def begin():
        twin_copy(0, 0).wait_recv()
        twin_copy(0, 1).wait_recv()
        own_sent(0)
        own_sent(1)
        for r in ORDER:
            if r == PARTS[part_of(r)][0]:
                far_wait(0, part_of(r))
            keep(0, r, (solved(0, r) - row_sum(r)).astype(BF16))
            send_row(0, r)
        for r in range(ROWS):
            out_start(0, r)

    def advance(n):
        products(n, mid_only)
        twin_copy(n, 0).wait_recv()
        twin_copy(n, 1).wait_recv()
        if n >= FINE:
            far_wait(n, 0)
        for r in ORDER:
            if n < FINE and r == PARTS[part_of(r)][0]:
                far_wait(n, part_of(r))
            base[r] = solved(n, r) - row_sum(r)
        if n == 2:
            halo_sent(2)

        def finish(r):
            current = base[r]
            for k, (row, c) in enumerate(PLACES):
                if row == r:
                    current = current - jnp.dot(dense[k], xb[n + 1][c], preferred_element_type=F32)
            keep(n, r, current.astype(BF16))
            send_row(n, r)

        def left():
            for r in reversed(range(HALF)):
                @when(has_left)
                def _(r=r):
                    to_right(n + 1, r).wait_recv()

                finish(r)

        def right():
            @when(has_right)
            def _():
                to_left(n + 1).wait_recv()

            for r in reversed(range(HALF, ROWS)):
                finish(r)

        @when(far_right)
        def _():
            left()
            right()

        @when(jnp.logical_not(far_right))
        def _():
            right()
            left()

        if n < STEPS - 1:
            for r in range(ROWS):
                out_start(n, r)

    def share(n):
        if n > 0:
            twin_sent(n - 1)
        for i, r in enumerate(ORDER):
            stage[n, i] = row_sum(r).astype(BF16)
            if i % HALF == HALF - 1:
                twin_copy(n, i // HALF).start()

    def merged(n, r):
        return row_sum(r) + twin_row(n, r)

    def merge(n):
        twin_copy(n, 0).wait_recv()
        if n > 0:
            mixed_sent(n - 1)

        @when(h == 5)
        def _():
            for i, r in enumerate(ORDER):
                if i == HALF:
                    twin_copy(n, 1).wait_recv()
                mixed[n, r] = merged(n, r).astype(BF16)
                tree_copy(n, r).start()

        for a, k, direct, via in ((3, 0, BY_THREE, BY_ONE), (7, 1, BY_ONE, BY_THREE)):
            @when(h == a)
            def _(k=k, direct=direct, via=via):
                for i, r in enumerate(direct):
                    if i == 2:
                        twin_copy(n, 1).wait_recv()
                    mixed[n, r] = merged(n, r).astype(BF16)
                    far_copy(n, k, r).start()
                for r in via:
                    tree_wait(n, via, r)
                    mixed[n, r] = (merged(n, r) + tree[n, via.index(r)].astype(F32)).astype(BF16)
                    far_copy(n, k, r).start()

    for i in range(3, len(loads)):
        load_wait(i)

    @when(march)
    def _():
        for i in range(2):
            march_load(i).wait()
        fold()

    @when(even)
    def _():
        pl.semaphore_wait(back_sem, 1)
        cross(2).wait_recv()
        own_sent(0)
        halo_start(2)

    own_wait()

    @when(march)
    def _():
        inside(2).start()
        inside(3).start()

    for n in range(STEPS):
        if n == 0:
            products(0)

            @when(march)
            def _():
                begin()
        else:
            @when(even)
            def _(n=n):
                halo_wait(n + 1)

            @when(upper)
            def _(n=n):
                inside(n + 1).wait_recv()

            @when(march)
            def _(n=n):
                advance(n)
                if n == 1:
                    inside(4).start()

            @when(jnp.logical_not(march))
            def _(n=n):
                products(n)

        @when(odd == 0)
        def _(n=n):
            share(n)

        @when(gate)
        def _(n=n):
            merge(n)

        if n == 0:
            @when(even)
            def _():
                inside(2).start()
                inside(3).start()

            @when((odd == 0) & (h + 2 <= h_last))
            def _():
                cross(4).start()

            @when(even)
            def _():
                cross(3).wait_recv()
                halo_sent(2)
                halo_start(3)

        if n == 1:
            @when(even)
            def _():
                inside(4).start()
                cross(4).wait_recv()
                halo_start(4)

    @when(first)
    def _():
        for i in range(len(loads)):
            swap(i).wait_send()

    @when(h == 0)
    def _():
        own_sent(0)
        own_sent(1)

    @when(lower)
    def _():
        halo_sent(3)
        halo_sent(4)
        for j in (2, 3, 4):
            inside(j).wait_send()

    @when((odd == 1) & (h < h_last))
    def _():
        cross(3).wait_send()

    @when((odd == 0) & (h + 2 <= h_last))
    def _():
        cross(4).wait_send()

    @when(odd == 0)
    def _():
        twin_sent(STEPS - 1)

    @when(gate)
    def _():
        mixed_sent(STEPS - 1)

    @when(march)
    def _():
        pltpu.make_async_copy(stage.at[0, pl.ds(0, STEPS)], out_ref, own_send).wait()
        remote(mixed.at[:, pl.ds(0, ROWS - 1)], mixed.at[:, pl.ds(0, ROWS - 1)], out_send, out_recv, at(hist=0)).wait_send()

    @when(jnp.logical_not(march))
    def _():
        remote(stage.at[0, pl.ds(0, STEPS)], out_ref, out_send, out_recv, at(hist=MARCH)).wait_recv()


def on_device(zblocks, slot_row, slot_offset, slot_delay, history, inverse, excite):
    _, cap, bs, _ = zblocks.shape
    columns = history.shape[2]
    slots = zblocks[0]
    past = history.reshape(history.shape[0], ROWS, bs, columns)
    inv = inverse.reshape(ROWS, bs, bs)
    exc = excite.reshape(STEPS, ROWS, bs, columns)
    operands = (slots, slot_row, slot_offset, slot_delay, past, inv, exc)
    any_spec = pl.BlockSpec(memory_space=pl.ANY)
    block = (bs, columns)
    dma = pltpu.SemaphoreType.DMA
    return pl.pallas_call(
        kernel,
        out_shape=pltpu.VMEM((STEPS, bs, columns), BF16),
        in_specs=[any_spec] * 7,
        out_specs=any_spec,
        scratch_shapes=[pltpu.VMEM((2, ROWS + 2 * R) + block, BF16)]
        + [pltpu.VMEM((ROWS + 2 * R,) + block, BF16) for _ in range(4)]
        + [
            pltpu.VMEM((ROWS,) + block, BF16),
            pltpu.VMEM((len(PLACES), bs, bs), BF16),
            pltpu.VMEM((cap, bs, bs), BF16),
            pltpu.VMEM((cap + 1,) + block, F32),
            pltpu.VMEM((STEPS, ROWS) + block, BF16),
            pltpu.VMEM((STEPS, ROWS) + block, BF16),
            pltpu.VMEM((STEPS, ROWS) + block, BF16),
            pltpu.VMEM((STEPS, len(BY_ONE)) + block, BF16),
            pltpu.VMEM((STEPS, 2, ROWS) + block, BF16),
            pltpu.VMEM((ROWS,) + block, F32),
            pltpu.VMEM((STEPS, ROWS) + block, BF16),
            pltpu.VMEM((ROWS, bs, bs), BF16),
            pltpu.SMEM((1, cap), jnp.int32),
            pltpu.SMEM((1, cap), jnp.int32),
            pltpu.SMEM((1, cap), jnp.int32),
            pltpu.SMEM((cap,), jnp.int32),
            pltpu.SMEM((cap,), jnp.int32),
            pltpu.SMEM((ROWS,), jnp.int32),
            pltpu.SMEM((cap,), jnp.int32),
            pltpu.SMEM((len(PLACES),), jnp.int32),
            pltpu.SemaphoreType.REGULAR,
            pltpu.SemaphoreType.REGULAR,
            dma((7,)),
            dma((5,)),
            dma((2, 2)),
            dma((4, 2)),
            dma((STEPS - 1, R)),
            dma((3,)),
            dma((3,)),
            dma,
            dma((STEPS, 2)),
            dma,
            dma((FINE, 2, HALF)),
            dma((STEPS - FINE, 2)),
            dma((FINE, len(BY_ONE))),
            dma((STEPS - FINE,)),
            dma,
            dma,
            dma,
        ],
        compiler_params=pltpu.CompilerParams(
            collective_id=0, has_side_effects=True, vmem_limit_bytes=60 * 1024 * 1024
        ),
    )(*[pltpu.with_memory_space_constraint(v, pltpu.HBM) for v in operands])


def solution(mesh):
    return jax.shard_map(
        on_device,
        mesh=mesh,
        in_specs=(
            P("hist", "patch", None, None),
            P("hist", "patch"),
            P("hist", "patch"),
            P("hist", "patch"),
            P("hist", "patch", None),
            P("patch", None),
            P(None, "patch", None),
        ),
        out_specs=P(None, ("patch", "hist"), None),
        check_vma=False,
    )
```
